256 devices in a mesh: rep: 8 (over y, core), dom: 32 (over z, x).
Axes of the slice: x: 4, y: 4, z: 8, core: 2. Of those that a mesh axis runs over, the one named last changes fastest.
Arguments:
- tile_values: bfloat16 [8, 32, 32, 2, 128, 128], P('rep', 'dom'), may hold values from -0.09375 to 0.09375
- tile_rows: int32 [8, 32, 32, 2], P('rep', 'dom'), may hold values from 0 to 1
- tile_cols: int32 [8, 32, 32, 2], P('rep', 'dom'), may hold values from 0 to 15
- tile_counts: int32 [8, 32, 32], P('rep', 'dom'), may hold values from 0 to 2
- features: bfloat16 [65536, 128], P(('dom', 'rep')), may hold values from -6 to 6
- weight_in: bfloat16 [128, 512], replicated, may hold values from -0.5 to 0.5
- weight_out: bfloat16 [512, 512], replicated, may hold values from -0.25 to 0.25
- cotangent: bfloat16 [65536, 512], P(('dom', 'rep')), may hold values from -0.0234375 to 0.0234375
Outputs:
- logits: bfloat16 [65536, 512], P(('dom', 'rep'))
- grad_in: float32 [128, 512], replicated
- grad_out: float32 [512, 512], replicated
The draws below stay inside these ranges and needn't reach their ends.
Inputs may be any that keep to these rules, and one draw needn't show every extreme that they name: `tile_counts`: slots at or after the count hold values that are not used.
All inputs are finite; a program needn't handle non-finite values.
Results may differ from the reference program's by a relative error of at most 0.018.
Values may be sent and summed in bfloat16 or wider, within the bound.
A program may use at most 128 MiB of HBM per device.

```python
import jax
import jax.numpy as jnp
from jax import lax

F_IN = 128
HID = 512
TILE = 128
CAP = 2
NODE_DEV = 256
NODES = 65536
N_REP = 8
N_DOM = 32


def place_ends(values, own_key, low, top_value):
    longest = values.shape.index(max(values.shape))
    spots = []
    for shift in (0, 1):
        where = [jax.random.randint(jax.random.fold_in(own_key, axis), (), 0, length) for axis, length in enumerate(values.shape)]
        where[longest] = (where[longest] + shift) % values.shape[longest]
        spots.append(tuple(where))
    return values.at[spots[0]].set(low).at[spots[1]].set(top_value)


def shard_levels(stream_key, extent, pieces, smallest, high):
    def one(axis_at, blocks):
        steps = jax.random.uniform(jax.random.fold_in(jax.random.fold_in(stream_key, 6), axis_at), (blocks,), jnp.float32, smallest / len(pieces), high / len(pieces))
        return jnp.repeat(jnp.exp(steps), extent[axis_at] // blocks).reshape((-1,) + (1,) * (len(extent) - axis_at - 1))

    loudness = one(*pieces[0])
    for cut in pieces[1:]:
        loudness = loudness * one(*cut)
    return loudness


def gaussian(key, dims, scale, reach, pieces=(), held_as=jnp.bfloat16):
    result = jax.random.normal(key, dims, jnp.float32) * scale
    if len(pieces) > 0:
        result = shard_levels(key, dims, pieces, -0.22, 0.18) * result
    return jnp.clip(result, min=-reach, max=reach).astype(held_as)


def setup_inputs(seed: int = 0) -> dict:
    splits = jax.random.split(jax.random.key(seed), 9)
    return {
        "tile_values": gaussian(splits[0], (N_REP, N_DOM, N_DOM, CAP, TILE, TILE), (TILE * N_DOM * CAP * TILE // NODE_DEV) ** -0.5, 0.09375, ((0, 8), (1, 32))),
        "tile_rows": place_ends(jax.random.randint(splits[1], (N_REP, N_DOM, N_DOM, CAP), 0, NODE_DEV // TILE), jax.random.fold_in(splits[1], 1), 0, (NODE_DEV // TILE) - 1).astype(jnp.int32),
        "tile_cols": place_ends(jax.random.randint(splits[2], (N_REP, N_DOM, N_DOM, CAP), 0, N_REP * NODE_DEV // TILE), jax.random.fold_in(splits[2], 1), 0, (N_REP * NODE_DEV // TILE) - 1).astype(jnp.int32),
        "tile_counts": place_ends(jax.random.randint(splits[3], (N_REP, N_DOM, N_DOM), 0, CAP + 1), jax.random.fold_in(splits[3], 1), 0, CAP).astype(jnp.int32),
        "features": gaussian(splits[4], (NODES, F_IN), 1.0, 6.0, ((0, 256),)),
        "weight_in": gaussian(splits[5], (F_IN, HID), F_IN ** -0.5, 0.5),
        "weight_out": gaussian(splits[6], (HID, HID), HID ** -0.5, 0.25),
        "cotangent": gaussian(splits[7], (NODES, HID), NODES ** -0.5, 0.0234375, ((0, 256),)),
    }


def silu_slope(value):
    sig = jax.nn.sigmoid(value)
    return sig * (1.0 + value * (1.0 - sig))


def reference(tile_values, tile_rows, tile_cols, tile_counts, features, weight_in, weight_out, cotangent):
    row_blocks = NODE_DEV // TILE
    col_blocks = N_REP * NODE_DEV // TILE
    live = jnp.arange(CAP)[None, None, None, :] < tile_counts[:, :, :, None]
    masked = jnp.where(live[..., None, None], tile_values, jnp.zeros_like(tile_values))
    order_tiles = jnp.swapaxes(masked, 0, 1).reshape(N_DOM * N_REP, N_DOM, CAP, TILE, TILE)
    order_rows = jnp.swapaxes(tile_rows, 0, 1).reshape(N_DOM * N_REP, N_DOM, CAP)
    order_cols = jnp.swapaxes(tile_cols, 0, 1).reshape(N_DOM * N_REP, N_DOM, CAP)
    block_index = jnp.arange(N_DOM)[:, None]

    def aggregate(values):
        width = values.shape[1]
        blocks = values.reshape(N_DOM, col_blocks, TILE, width)

        def one(args):
            tiles, rows, cols = args
            picked = blocks[block_index, cols]
            prod = jnp.einsum("sktu,skuf->sktf", tiles.astype(jnp.float32), picked.astype(jnp.float32)).astype(jnp.bfloat16)
            table = (rows[:, :, None] == jnp.arange(row_blocks)[None, None, :]).astype(jnp.float32)
            return jnp.einsum("skb,sktf->btf", table, prod.astype(jnp.float32)).reshape(NODE_DEV, width)

        summed = lax.map(one, (order_tiles, order_rows, order_cols))
        return summed.reshape(NODES, width).astype(jnp.bfloat16)

    agg1 = aggregate(features)
    z1 = jnp.dot(agg1, weight_in, preferred_element_type=jnp.float32)
    hidden = jax.nn.silu(z1).astype(jnp.bfloat16)
    agg2 = aggregate(hidden)
    logits = jnp.dot(agg2, weight_out, preferred_element_type=jnp.float32).astype(jnp.bfloat16)
    dagg = jnp.dot(cotangent, weight_out.T, preferred_element_type=jnp.float32).astype(jnp.bfloat16)
    grad_out = jnp.dot(agg2.T, cotangent, preferred_element_type=jnp.float32)
    dagg_blocks = dagg.reshape(N_DOM, N_REP, row_blocks, TILE, HID)
    dh = jnp.zeros((N_DOM, col_blocks, TILE, HID), jnp.float32)
    for rank in range(N_REP):
        def step(total, args):
            tiles, rows, cols, mine = args
            taken = mine[rows]
            terms = jnp.einsum("sktu,sktf->skuf", tiles.astype(jnp.float32), taken.astype(jnp.float32)).astype(jnp.bfloat16)
            total = total.at[block_index, cols].add(terms.astype(jnp.float32))
            return total, 0

        start = jnp.zeros((N_DOM, col_blocks, TILE, HID), jnp.float32)
        total, _ = lax.scan(step, start, (masked[rank], tile_rows[rank], tile_cols[rank], dagg_blocks[:, rank]))
        rounded = lax.optimization_barrier(total.astype(jnp.bfloat16))
        dh = dh + rounded.astype(jnp.float32)
    dh = dh.reshape(NODES, HID)
    dz = (dh * silu_slope(z1)).astype(jnp.bfloat16)
    grad_in = jnp.dot(agg1.T, dz, preferred_element_type=jnp.float32)
    return logits, grad_in, grad_out
```

```python
import jax
import jax.numpy as jnp
from jax import lax
from jax.sharding import PartitionSpec as P


def route(values):
    return lax.all_to_all(values, "dom", split_axis=0, concat_axis=0, tiled=True)


def dot(a, b, ca, cb):
    return lax.dot_general(a, b, (((ca,), (cb,)), ((), ())), preferred_element_type=jnp.float32)


def per_device(
    tile_values, tile_rows, tile_cols, tile_counts, features, weight_in, weight_out, cotangent
):
    tiles = tile_values[0, 0]
    rows = tile_rows[0, 0]
    cols = tile_cols[0, 0]
    counts = tile_counts[0, 0]
    width = tiles.shape[-1]
    slots = tiles.shape[1]
    node_rows = features.shape[0]
    row_blocks = node_rows // width
    col_blocks = lax.axis_size("rep") * node_rows // width
    live = jnp.arange(slots)[None, :] < counts[:, None]
    here = live[None] & (rows[None] == jnp.arange(row_blocks)[:, None, None])
    spread = jnp.where(here[:, :, :, None, None], tiles[None], jnp.zeros_like(tiles)[None])
    spread = jnp.transpose(spread, (0, 3, 1, 2, 4)).reshape(node_rows, -1)
    far_cols = route(cols)

    def fetch(values):
        block = lax.all_gather(values, "rep", axis=0, tiled=True)
        picked = block.reshape(col_blocks, width, values.shape[1])[far_cols]
        return route(picked).reshape(-1, values.shape[1])

    agg1 = dot(spread, fetch(features), 1, 0).astype(jnp.bfloat16)
    near = fetch(agg1)
    z1 = dot(near, weight_in, 1, 0)
    sig = 0.5 + 0.5 * jnp.tanh(0.5 * z1)
    hidden = z1 * sig
    slope = sig + hidden * (1.0 - sig)
    agg2 = dot(spread, hidden.astype(jnp.bfloat16), 1, 0).astype(jnp.bfloat16)
    logits = dot(agg2, weight_out, 1, 0).astype(jnp.bfloat16)
    dagg = dot(cotangent, weight_out, 1, 1).astype(jnp.bfloat16)
    dz = (dot(spread, dagg, 0, 0) * slope).astype(jnp.bfloat16)
    term_in = dot(near, dz, 0, 0)
    term_out = dot(agg2, cotangent, 0, 0)
    grad_in, grad_out = lax.psum((term_in, term_out), ("rep", "dom"))
    return (logits, grad_in, grad_out)


def solution(mesh):
    placed = (
        P("rep", "dom", None, None, None, None),
        P("rep", "dom", None, None),
        P("rep", "dom", None, None),
        P("rep", "dom", None),
        P(("dom", "rep"), None),
        P(),
        P(),
        P(("dom", "rep"), None),
    )
    return jax.shard_map(
        per_device,
        mesh=mesh,
        in_specs=placed,
        out_specs=(P(("dom", "rep"), None), P(), P()),
        check_vma=False,
    )
```

```python
import functools

import jax
import jax.numpy as jnp
from jax import lax
from jax.experimental import pallas as pl
from jax.experimental.pallas import tpu as pltpu
from jax.sharding import PartitionSpec as P

BF = jnp.bfloat16
F32 = jnp.float32

NY, NK, NZ, NX = 4, 2, 8, 4
NR = NY * NK
ND = NZ * NX
SLOTS = 2
TILE = 128
OWN = 2
BLOCKS = NR * OWN
HALF = BLOCKS // NK
STEPS = NZ // 2
GROUPS = NZ
PLANE = NY * NX
LANES = 640
CHUNK = 16
CHUNKS = 512 // CHUNK
SHARE = CHUNKS // NK

OFFSET = [0] + [s * t for t in range(1, STEPS) for s in (-1, 1)] + [STEPS]


def group_of(way, step):
    if step == 0:
        return 0
    if step == STEPS:
        return GROUPS - 1
    return 2 * step - 1 + way


def dot(a, b, ca, cb):
    return lax.dot_general(a, b, (((ca,), (cb,)), ((), ())), preferred_element_type=F32)


def kernel(*refs):
    refs = list(refs)

    def take(n):
        out, refs[:n] = refs[:n], []
        return out

    tiles, rows_s, cols_s, counts_s, cols_v, feat, w_in, w_out, cot = take(9)
    logits, grad_in, grad_out = take(3)
    raw = [take(GROUPS), take(GROUPS)]
    picked = take(2)
    sending = take(2)
    far_v, far_s, spread, w_in_t, dagg_t, acc1, agg1, acc2, acc3 = take(9)
    part, red1_out, red1_in, red2_out, red2_in, red3, full = take(7)
    a_s, a_r, b_s, b_r, p_s, p_r, c_s, c_r, col_s, col_r, loc = take(11)
    g1_s, g1_r, g2_s, g2_r, g3_s, g3_r, g4_s, g4_r, g5_s, g5_r = take(10)

    r = lax.axis_index("rep")
    d = lax.axis_index("dom")
    y, k = r // NK, r % NK
    z, x = d // NX, d % NX
    left = []

    def send(src, dst, s_sem, r_sem, rr, zz, xx):
        copy = pltpu.make_async_remote_copy(
            src_ref=src,
            dst_ref=dst,
            send_sem=s_sem,
            recv_sem=r_sem,
            device_id=(rr, zz * NX + xx),
            device_id_type=pl.DeviceIdType.MESH,
        )
        copy.start()
        left.append(copy)
        return copy

    greet = [((r + i) % NR, z, x) for i in range(1, NR)]
    for dx in range(1, NX):
        for dy in range(NY):
            greet.append((((y + dy) % NY) * NK + k, z, (x + dx) % NX))
    for dz in range(1, NZ):
        greet.append((r, (z + dz) % NZ, x))
    barrier = pltpu.get_barrier_semaphore()
    for rr, zz, xx in greet:
        pl.semaphore_signal(
            barrier, inc=1, device_id=(rr, zz * NX + xx), device_id_type=pl.DeviceIdType.MESH
        )
    pl.semaphore_wait(barrier, len(greet))

    def gather_rep(p, own):
        copies = []
        for i in range(1, NR):
            copies.append(
                send(
                    own,
                    raw[p][0].at[pl.ds(OWN * r, OWN)],
                    a_s.at[p, i - 1],
                    a_r.at[p, i - 1],
                    (r + i) % NR,
                    z,
                    x,
                )
            )
        raw[p][0][pl.ds(OWN * r, OWN)] = own[...]
        return copies

    def ring(p, way, step):
        if step < STEPS:
            where = pl.ds(HALF * k, HALF)
        else:
            where = pl.ds(HALF * k + way * (HALF // 2), HALF // 2)
        return send(
            raw[p][group_of(way, step - 1)].at[where],
            raw[p][group_of(way, step)].at[where],
            b_s.at[p, way, step - 1],
            b_r.at[p, way, step - 1],
            r,
            (z + (1, NZ - 1)[way]) % NZ,
            x,
        )

    def share(p, g):
        where = pl.ds(HALF * k, HALF)
        return send(
            raw[p][g].at[where],
            raw[p][g].at[where],
            p_s.at[p, g - 1],
            p_r.at[p, g - 1],
            y * NK + 1 - k,
            z,
            x,
        )

    def pick(p, g):
        c = ((z + OFFSET[g] + NZ) % NZ) * NX + x
        copies = []
        for dx in range(1, NX):
            for s in range(SLOTS):
                j = far_s[dx - 1, 0, c * SLOTS + s]
                sending[p][g, dx - 1, s] = raw[p][g][j]
            copies.append(
                send(
                    sending[p].at[g, dx - 1],
                    picked[p].at[g, x],
                    c_s.at[p, g, dx - 1],
                    c_r.at[p, g, dx - 1],
                    r,
                    z,
                    (x + dx) % NX,
                )
            )
        for s in range(SLOTS):
            picked[p][g, x, s] = raw[p][g][cols_s[c * SLOTS + s]]
        return copies

    def exchange(p, own, early, meanwhile, consume):
        copies = gather_rep(p, own)
        early()
        for copy in copies:
            copy.wait_recv()
        going = [ring(p, 0, 1), ring(p, 1, 1)]
        coming = [(0, pick(p, 0))]
        meanwhile()
        for step in range(1, STEPS + 1):
            shares = []
            later = []
            if step < STEPS:
                for way in (0, 1):
                    going[way].wait_recv()
                    later.append(ring(p, way, step + 1))
                    g = group_of(way, step)
                    shares.append((g, share(p, g)))
            else:
                going[0].wait_recv()
                going[1].wait_recv()
                shares.append((GROUPS - 1, share(p, GROUPS - 1)))
            going = later
            fresh = []
            for g, copy in shares:
                copy.wait_recv()
                fresh.append((g, pick(p, g)))
            for g, copies in coming:
                for copy in copies:
                    copy.wait_recv()
                consume(g)
            coming = fresh
        for g, copies in coming:
            for copy in copies:
                copy.wait_recv()
            consume(g)

    col_copies = [
        send(cols_v, far_v.at[dx - 1], col_s.at[dx - 1], col_r.at[dx - 1], r, z, (x + NX - dx) % NX)
        for dx in range(1, NX)
    ]

    def early1():
        for copy in col_copies:
            copy.wait_recv()
        local = pltpu.make_async_copy(far_v, far_s, loc.at[0])
        local.start()
        local.wait()

    def meanwhile1():
        for g in range(GROUPS):
            zc = (z + OFFSET[g] + NZ) % NZ

            def place(xc, carry, g=g, zc=zc):
                c = zc * NX + xc
                for s in range(SLOTS):
                    tile = tiles[c, s]
                    row = rows_s[c * SLOTS + s]
                    live = s < counts_s[c]
                    for b in range(OWN):
                        spread[g * NX + xc, b * TILE : (b + 1) * TILE, s * TILE : (s + 1) * TILE] = (
                            jnp.where(jnp.logical_and(live, row == b), tile, jnp.zeros_like(tile))
                        )
                return carry

            lax.fori_loop(0, NX, place, 0)
        w_in_t[...] = w_in[...].astype(F32).T.astype(BF)
        dagg_t[...] = dot(w_out[...], cot[...], 1, 1).astype(BF)
        acc1[...] = jnp.zeros_like(acc1)
        acc2[...] = jnp.zeros_like(acc2)
        acc3[...] = jnp.zeros_like(acc3)

    def consume1(g):
        def body(xc, carry):
            near = picked[0][g, xc].reshape(SLOTS * TILE, TILE)
            acc1[...] += dot(spread[g * NX + xc], near, 1, 0)
            return carry

        lax.fori_loop(0, NX, body, 0)

    exchange(0, feat, early1, meanwhile1, consume1)
    agg1[...] = acc1[...].astype(BF).reshape(OWN, TILE, TILE)

    def consume2(g):
        def body(xc, carry):
            near = picked[1][g, xc].reshape(SLOTS * TILE, TILE)
            tile = spread[g * NX + xc]
            z1 = dot(w_in_t[...], near, 1, 1)
            sig = 0.5 + 0.5 * jnp.tanh(0.5 * z1)
            hidden = z1 * sig
            slope = sig + hidden * (1.0 - sig)
            acc2[...] += dot(hidden.astype(BF), tile, 1, 1)
            dz = (dot(dagg_t[...], tile, 1, 0) * slope).astype(BF)
            acc3[...] += dot(dz, near, 1, 0)
            return carry

        lax.fori_loop(0, NX, body, 0)

    exchange(1, agg1, lambda: None, lambda: None, consume2)

    agg2_t = acc2[...].astype(BF)
    part[:, :, 0:512] = dot(agg2_t, cot[...], 1, 0).reshape(CHUNKS, CHUNK, 512)
    part[:, :, 512:LANES] = acc3[...].reshape(CHUNKS, CHUNK, TILE)

    mine = pl.ds(SHARE * k, SHARE)
    red1_out[...] = part[pl.ds(SHARE * (1 - k), SHARE)].astype(BF)
    copy = send(red1_out, red1_in, g1_s.at[0], g1_r.at[0], y * NK + 1 - k, z, x)
    logits[...] = dot(agg2_t, w_out[...], 0, 0).astype(BF)
    copy.wait_recv()
    red2_out[...] = (part[mine] + red1_in[...].astype(F32)).astype(BF)
    me = y * NX + x
    plane = [(dy, dx) for dy in range(NY) for dx in range(NX) if dy or dx]
    copies = []
    for i, (dy, dx) in enumerate(plane):
        yy, xx = (y + dy) % NY, (x + dx) % NX
        copies.append(
            send(red2_out.at[yy * NX + xx], red2_in.at[i], g2_s.at[i], g2_r.at[i], yy * NK + k, z, xx)
        )
    for copy in copies:
        copy.wait_recv()
    total = red2_out[me].astype(F32)
    for i in range(PLANE - 1):
        total = total + red2_in[i].astype(F32)
    red3[z] = total.astype(BF)
    copies = [
        send(red3.at[z], red3.at[z], g3_s.at[i - 1], g3_r.at[i - 1], r, (z + i) % NZ, x)
        for i in range(1, NZ)
    ]
    for copy in copies:
        copy.wait_recv()
    total = red3[0].astype(F32)
    for i in range(1, NZ):
        total = total + red3[i].astype(F32)
    full[SHARE * k + me] = total.astype(BF)
    copies = []
    for i, (dy, dx) in enumerate(plane):
        yy, xx = (y + dy) % NY, (x + dx) % NX
        at = full.at[SHARE * k + me]
        copies.append(send(at, at, g4_s.at[i], g4_r.at[i], yy * NK + k, z, xx))
    for copy in copies:
        copy.wait_recv()
    copy = send(full.at[mine], full.at[mine], g5_s.at[0], g5_r.at[0], y * NK + 1 - k, z, x)
    copy.wait_recv()
    grad_out[...] = full[:, :, 0:512].astype(F32).reshape(512, 512)
    grad_in[...] = full[:, :, 512:LANES].astype(F32).reshape(512, TILE).T
    for copy in left:
        copy.wait_send()


def per_device(
    tile_values, tile_rows, tile_cols, tile_counts, features, weight_in, weight_out, cotangent
):
    cols = tile_cols.reshape(ND * SLOTS)
    cols_v = jnp.pad(cols.reshape(1, ND * SLOTS), ((0, 7), (0, TILE - ND * SLOTS)))
    vmem = pl.BlockSpec(memory_space=pltpu.VMEM)
    smem = pl.BlockSpec(memory_space=pltpu.SMEM)
    block = pltpu.VMEM((BLOCKS, TILE, TILE), BF)
    dma = pltpu.SemaphoreType.DMA
    scratch = [block] * (2 * GROUPS)
    scratch += [pltpu.VMEM((GROUPS, NX, SLOTS, TILE, TILE), BF)] * 2
    scratch += [pltpu.VMEM((GROUPS, NX - 1, SLOTS, TILE, TILE), BF)] * 2
    scratch += [
        pltpu.VMEM((NX - 1, 8, TILE), jnp.int32),
        pltpu.SMEM((NX - 1, 8, TILE), jnp.int32),
        pltpu.VMEM((ND, 256, 256), BF),
        pltpu.VMEM((512, TILE), BF),
        pltpu.VMEM((512, 256), BF),
        pltpu.VMEM((256, TILE), F32),
        pltpu.VMEM((OWN, TILE, TILE), BF),
        pltpu.VMEM((512, 256), F32),
        pltpu.VMEM((512, TILE), F32),
        pltpu.VMEM((CHUNKS, CHUNK, LANES), F32),
        pltpu.VMEM((SHARE, CHUNK, LANES), BF),
        pltpu.VMEM((SHARE, CHUNK, LANES), BF),
        pltpu.VMEM((SHARE, CHUNK, LANES), BF),
        pltpu.VMEM((PLANE - 1, CHUNK, LANES), BF),
        pltpu.VMEM((NZ, CHUNK, LANES), BF),
        pltpu.VMEM((CHUNKS, CHUNK, LANES), BF),
    ]
    for shape in (
        (2, NR - 1),
        (2, 2, STEPS),
        (2, GROUPS - 1),
        (2, GROUPS, NX - 1),
        (NX - 1,),
    ):
        scratch += [dma(shape)] * 2
    scratch += [dma((1,))]
    for count in (1, PLANE - 1, NZ - 1, PLANE - 1, 1):
        scratch += [dma((count,))] * 2
    logits, grad_in, grad_out = pl.pallas_call(
        kernel,
        out_shape=(
            jax.ShapeDtypeStruct((256, 512), BF),
            jax.ShapeDtypeStruct((TILE, 512), F32),
            jax.ShapeDtypeStruct((512, 512), F32),
        ),
        in_specs=[vmem, smem, smem, smem] + [vmem] * 5,
        out_specs=(vmem,) * 3,
        scratch_shapes=scratch,
        compiler_params=pltpu.CompilerParams(
            collective_id=0, has_side_effects=True, vmem_limit_bytes=48 * 1024 * 1024
        ),
        cost_estimate=pl.CostEstimate(
            flops=5_000_000_000, bytes_accessed=5_000_000, transcendentals=4_000_000
        ),
    )(
        tile_values.reshape(ND, SLOTS, TILE, TILE),
        tile_rows.reshape(ND * SLOTS),
        cols,
        tile_counts.reshape(ND),
        cols_v,
        features.reshape(OWN, TILE, TILE),
        weight_in,
        weight_out,
        cotangent,
    )
    return logits, grad_in, grad_out


def solution(mesh):
    placed = (
        P("rep", "dom", None, None, None, None),
        P("rep", "dom", None, None),
        P("rep", "dom", None, None),
        P("rep", "dom", None),
        P(("dom", "rep"), None),
        P(),
        P(),
        P(("dom", "rep"), None),
    )
    return jax.shard_map(
        per_device,
        mesh=mesh,
        in_specs=placed,
        out_specs=(P(("dom", "rep"), None), P(), P()),
        check_vma=False,
    )
```

```python
import jax
import jax.numpy as jnp
from jax import lax
from jax.experimental import pallas as pl
from jax.experimental.pallas import tpu as pltpu
from jax.sharding import PartitionSpec as P

BF = jnp.bfloat16
F32 = jnp.float32

NY, NK, NZ, NX = 4, 2, 8, 4
NR = NY * NK
ND = NZ * NX
SLOTS = 2
TILE = 128
OWN = 2
BLOCKS = NR * OWN
HALF = BLOCKS // NK
STEPS = NZ // 2
GROUPS = NZ
PLANE = NY * NX
LANES = 640
CHUNK = 16
CHUNKS = 512 // CHUNK
SHARE = CHUNKS // NK

OFFSET = [0] + [s * t for t in range(1, STEPS) for s in (-1, 1)] + [STEPS]


def group_of(way, step):
    if step == 0:
        return 0
    if step == STEPS:
        return GROUPS - 1
    return 2 * step - 1 + way


def dot(a, b, ca, cb):
    return lax.dot_general(a, b, (((ca,), (cb,)), ((), ())), preferred_element_type=F32)


def kernel(*refs):
    refs = list(refs)

    def take(n):
        out, refs[:n] = refs[:n], []
        return out

    tiles_h, rows_h, cols_h, counts_h, feat, w_in_h, w_out_h, cot_h = take(8)
    logits_h, full_h = take(2)
    raw = [take(GROUPS), take(GROUPS)]
    picked = take(2)
    sending = take(2)
    tiles, w_in, w_out, cot, rows_s, cols_s, counts_s = take(7)
    far_v, far_s, spread, w_in_t, dagg_t, acc1, agg1, acc2, acc3 = take(9)
    agg2_t, logits, red1_out, red1_in, red2_out, red2_in, red3, full = take(8)
    y_s, y_r, b_s, b_r, p_s, p_r, c_s, c_r, col_s, col_r, loc = take(11)
    g1_s, g1_r, g2_s, g2_r, g3_s, g3_r, g4_s, g4_r, g5_s, g5_r = take(10)

    r = lax.axis_index("rep")
    d = lax.axis_index("dom")
    y, k = r // NK, r % NK
    z, x = d // NX, d % NX
    left = []

    def send(src, dst, s_sem, r_sem, rr, zz, xx):
        copy = pltpu.make_async_remote_copy(
            src_ref=src,
            dst_ref=dst,
            send_sem=s_sem,
            recv_sem=r_sem,
            device_id=(rr, zz * NX + xx),
            device_id_type=pl.DeviceIdType.MESH,
        )
        copy.start()
        left.append(copy)
        return copy

    def fetch(i, src, dst):
        copy = pltpu.make_async_copy(src, dst, loc.at[i])
        copy.start()
        return copy

    small = [fetch(0, cols_h, cols_s), fetch(1, rows_h, rows_s), fetch(2, counts_h, counts_s)]
    large = [
        fetch(3, tiles_h, tiles),
        fetch(4, w_in_h, w_in),
        fetch(5, w_out_h, w_out),
        fetch(6, cot_h, cot),
    ]

    greet = [(y * NK + 1 - k, z, x)]
    for dx in range(NX):
        for dy in range(NY):
            if dx or dy:
                greet.append((((y + dy) % NY) * NK + k, z, (x + dx) % NX))
    for dz in range(1, NZ):
        greet.append((r, (z + dz) % NZ, x))
    barrier = pltpu.get_barrier_semaphore()
    for rr, zz, xx in greet:
        pl.semaphore_signal(
            barrier, inc=1, device_id=(rr, zz * NX + xx), device_id_type=pl.DeviceIdType.MESH
        )
    pl.semaphore_wait(barrier, len(greet))

    half = pl.ds(HALF * k, HALF)
    at = HALF * k + OWN * y

    def ring(p, own, way, step):
        first, count = (0, OWN) if step < STEPS else (way, 1)
        here = pl.ds(at + first, count)
        src = own if step == 1 else raw[p][group_of(way, step - 1)].at[here]
        return send(
            src,
            raw[p][group_of(way, step)].at[here],
            b_s.at[p, way, step - 1],
            b_r.at[p, way, step - 1],
            r,
            (z + (1, NZ - 1)[way]) % NZ,
            x,
        )

    def gather_y(p, own, g):
        here = pl.ds(at, OWN)
        return [
            send(
                own if g == 0 else raw[p][g].at[here],
                raw[p][g].at[here],
                y_s.at[p, g, dy - 1],
                y_r.at[p, g, dy - 1],
                ((y + dy) % NY) * NK + k,
                z,
                x,
            )
            for dy in range(1, NY)
        ]

    def relay(p, way, i):
        here = pl.ds(HALF * k + OWN * ((y + NY - i) % NY), OWN)
        g = group_of(way, 2)
        return send(
            raw[p][group_of(way, 1)].at[here],
            raw[p][g].at[here],
            y_s.at[p, g, i - 1],
            y_r.at[p, g, i - 1],
            r,
            (z + (1, NZ - 1)[way]) % NZ,
            x,
        )

    def share(p, g):
        return send(
            raw[p][g].at[half],
            raw[p][g].at[half],
            p_s.at[p, g],
            p_r.at[p, g],
            y * NK + 1 - k,
            z,
            x,
        )

    def block(p, g, j):
        return raw[p][g][((j >> 1) & 1) * HALF + (j >> 2) * OWN + (j & 1)]

    def pick(p, g):
        c = ((z + OFFSET[g] + NZ) % NZ) * NX + x
        copies = []
        for dx in (2, 1, 3):
            for s in range(SLOTS):
                sending[p][g, dx - 1, s] = block(p, g, far_s[dx - 1, s, c])
            copies.append(
                send(
                    sending[p].at[g, dx - 1],
                    picked[p].at[g, x],
                    c_s.at[p, g, dx - 1],
                    c_r.at[p, g, dx - 1],
                    r,
                    z,
                    (x + dx) % NX,
                )
            )
        for s in range(SLOTS):
            picked[p][g, x, s] = block(p, g, cols_s[s, c])
        return copies

    def exchange(p, own, keep, ready, early, meanwhile, consume):
        rings = {0: [ring(p, own, 0, 1), ring(p, own, 1, 1)]}
        ys = {0: gather_y(p, own, 0)}
        shares, picks = {}, {}
        keep()

        def do_z(step):
            for copy in rings[step - 1]:
                copy.wait_recv()
            if step < STEPS:
                rings[step] = [ring(p, own, 0, step + 1), ring(p, own, 1, step + 1)]
            for g in sorted({group_of(0, step), group_of(1, step)}):
                if step != 2:
                    ys[g] = gather_y(p, own, g)

        def do_y(g):
            for i, copy in enumerate(ys[g]):
                copy.wait_recv()
                if g in (1, 2):
                    ys.setdefault(g + 2, []).append(relay(p, g - 1, i + 1))
            if g == 0:
                ready()
            shares[g] = share(p, g)

        def do_k(g):
            shares[g].wait_recv()
            picks[g] = pick(p, g)

        def do_c(g):
            for copy in picks[g]:
                copy.wait_recv()

            def body(xc, carry):
                consume(g, xc)
                return carry

            lax.fori_loop(0, NX, body, 0)

        def do_last(g):
            consume(g, x)
            for dx, i in ((1, 1), (3, 2), (2, 0)):
                picks[g][i].wait_recv()
                consume(g, (x + NX - dx) % NX)

        meanwhile()
        do_z(1)
        do_y(0)
        early()
        do_k(0)
        do_z(2)
        do_y(1)
        do_k(1)
        do_z(3)
        do_y(2)
        do_k(2)
        do_c(0)
        do_y(3)
        do_z(4)
        do_k(3)
        do_c(1)
        do_y(5)
        do_k(5)
        do_c(2)
        do_y(4)
        do_k(4)
        do_c(3)
        do_y(6)
        do_k(6)
        do_c(5)
        do_y(7)
        do_k(7)
        do_c(4)
        do_c(6)
        do_last(7)

    col_copies = [
        send(cols_h, far_v.at[dx - 1], col_s.at[dx - 1], col_r.at[dx - 1], r, z, (x + NX - dx) % NX)
        for dx in range(1, NX)
    ]

    def early1():
        for copy in col_copies:
            copy.wait_recv()
        fetch(7, far_v, far_s).wait()

    kept = []

    def keep1():
        kept.append(fetch(8, feat, raw[0][0].at[pl.ds(at, OWN)]))

    def ready1():
        kept[0].wait()

    def keep2():
        raw[1][0][pl.ds(at, OWN)] = agg1[...]

    def meanwhile1():
        for copy in small + large:
            copy.wait()
        for g in range(GROUPS):
            zc = (z + OFFSET[g] + NZ) % NZ

            def place(xc, carry, g=g, zc=zc):
                c = zc * NX + xc
                for s in range(SLOTS):
                    tile = tiles[c, s]
                    row = rows_s[s, c]
                    live = s < counts_s[c]
                    for b in range(OWN):
                        spread[g * NX + xc, b * TILE : (b + 1) * TILE, s * TILE : (s + 1) * TILE] = (
                            jnp.where(jnp.logical_and(live, row == b), tile, jnp.zeros_like(tile))
                        )
                return carry

            lax.fori_loop(0, NX, place, 0)
        w_in_t[...] = w_in[...].astype(F32).T.astype(BF)
        dagg_t[...] = dot(w_out[...], cot[...], 1, 1).astype(BF)
        acc1[...] = jnp.zeros_like(acc1)
        acc2[...] = jnp.zeros_like(acc2)
        acc3[...] = jnp.zeros_like(acc3)

    def consume1(g, xc):
        near = picked[0][g, xc].reshape(SLOTS * TILE, TILE)
        acc1[...] += dot(spread[g * NX + xc], near, 1, 0)

    exchange(0, feat, keep1, ready1, early1, meanwhile1, consume1)
    agg1[...] = acc1[...].astype(BF).reshape(OWN, TILE, TILE)

    def consume2(g, xc):
        near = picked[1][g, xc].reshape(SLOTS * TILE, TILE)
        tile = spread[g * NX + xc]
        z1 = dot(w_in_t[...], near, 1, 1)
        sig = 0.5 + 0.5 * jnp.tanh(0.5 * z1)
        hidden = z1 * sig
        slope = sig + hidden * (1.0 - sig)
        acc2[...] += dot(hidden.astype(BF), tile, 1, 1)
        dz = (dot(dagg_t[...], tile, 1, 0) * slope).astype(BF)
        acc3[...] += dot(dz, near, 1, 0)

    def nothing():
        pass

    exchange(1, agg1, keep2, nothing, nothing, nothing, consume2)

    agg2_t[...] = acc2[...].astype(BF)

    def term(core):
        rows = pl.ds(256 * core, 256)
        return (
            dot(agg2_t[rows], cot[...], 1, 0).reshape(SHARE, CHUNK, 512),
            acc3[rows].reshape(SHARE, CHUNK, TILE),
        )

    out, back = term(1 - k)
    red1_out[:, :, 0:512] = out.astype(BF)
    red1_out[:, :, 512:LANES] = back.astype(BF)
    copy = send(red1_out, red1_in, g1_s.at[0], g1_r.at[0], y * NK + 1 - k, z, x)
    out, back = term(k)
    copy.wait_recv()
    red2_out[:, :, 0:512] = (out + red1_in[:, :, 0:512].astype(F32)).astype(BF)
    red2_out[:, :, 512:LANES] = (back + red1_in[:, :, 512:LANES].astype(F32)).astype(BF)
    me = y * NX + x
    plane = [(dy, dx) for dy in range(NY) for dx in range(NX) if dy or dx]
    plane.sort(key=lambda step: -min(step[0], NY - step[0]) - min(step[1], NX - step[1]))
    copies = []
    for i, (dy, dx) in enumerate(plane):
        yy, xx = (y + dy) % NY, (x + dx) % NX
        copies.append(
            send(red2_out.at[yy * NX + xx], red2_in.at[i], g2_s.at[i], g2_r.at[i], yy * NK + k, z, xx)
        )
    logits[...] = dot(agg2_t[...], w_out[...], 0, 0).astype(BF)
    done = fetch(0, logits, logits_h)
    total = red2_out[me].astype(F32)
    for i in range(PLANE - 2, -1, -1):
        copies[i].wait_recv()
        total = total + red2_in[i].astype(F32)
    red3[z] = total.astype(BF)
    copies = [
        send(red3.at[z], red3.at[z], g3_s.at[i - 1], g3_r.at[i - 1], r, (z + i) % NZ, x)
        for i in (4, 3, 5, 2, 6, 1, 7)
    ]
    for copy in copies:
        copy.wait_recv()
    total = red3[0].astype(F32)
    for i in range(1, NZ):
        total = total + red3[i].astype(F32)

    def to_core(i, chunk):
        return send(chunk, chunk, g5_s.at[i], g5_r.at[i], y * NK + 1 - k, z, x)

    full[SHARE * k + me] = total.astype(BF)
    chunk = full.at[SHARE * k + me]
    copies = []
    for i, (dy, dx) in enumerate(plane):
        yy, xx = (y + dy) % NY, (x + dx) % NX
        copies.append(send(chunk, chunk, g4_s.at[i], g4_r.at[i], yy * NK + k, z, xx))
    others = [to_core(PLANE - 1, chunk)]
    for i in range(PLANE - 2, -1, -1):
        copies[i].wait_recv()
        dy, dx = plane[i]
        came = ((y + NY - dy) % NY) * NX + (x + NX - dx) % NX
        others.append(to_core(i, full.at[SHARE * k + came]))
    for copy in others:
        copy.wait_recv()
    last = fetch(1, full, full_h)
    for copy in left:
        copy.wait_send()
    done.wait()
    last.wait()


def unpack(logits_in, full, logits, grad_in, grad_out):
    logits[...] = logits_in[...]
    grad_out[...] = full[:, :, 0:512].astype(F32).reshape(512, 512)
    grad_in[...] = full[:, :, 512:LANES].astype(F32).reshape(512, TILE).T


def per_device(
    tile_values, tile_rows, tile_cols, tile_counts, features, weight_in, weight_out, cotangent
):
    vmem = pl.BlockSpec(memory_space=pltpu.VMEM)
    hbm = pl.BlockSpec(memory_space=pltpu.HBM)
    block = pltpu.VMEM((BLOCKS, TILE, TILE), BF)
    dma = pltpu.SemaphoreType.DMA
    scratch = [block] * (2 * GROUPS)
    scratch += [pltpu.VMEM((GROUPS, NX, SLOTS, TILE, TILE), BF)] * 2
    scratch += [pltpu.VMEM((GROUPS, NX - 1, SLOTS, TILE, TILE), BF)] * 2
    scratch += [
        pltpu.VMEM((ND, SLOTS, TILE, TILE), BF),
        pltpu.VMEM((TILE, 512), BF),
        pltpu.VMEM((512, 512), BF),
        pltpu.VMEM((256, 512), BF),
        pltpu.SMEM((SLOTS, ND), jnp.int32),
        pltpu.SMEM((SLOTS, ND), jnp.int32),
        pltpu.SMEM((ND,), jnp.int32),
        pltpu.VMEM((NX - 1, SLOTS, ND), jnp.int32),
        pltpu.SMEM((NX - 1, SLOTS, ND), jnp.int32),
        pltpu.VMEM((ND, 256, 256), BF),
        pltpu.VMEM((512, TILE), BF),
        pltpu.VMEM((512, 256), BF),
        pltpu.VMEM((256, TILE), F32),
        pltpu.VMEM((OWN, TILE, TILE), BF),
        pltpu.VMEM((512, 256), F32),
        pltpu.VMEM((512, TILE), F32),
        pltpu.VMEM((512, 256), BF),
        pltpu.VMEM((256, 512), BF),
        pltpu.VMEM((SHARE, CHUNK, LANES), BF),
        pltpu.VMEM((SHARE, CHUNK, LANES), BF),
        pltpu.VMEM((SHARE, CHUNK, LANES), BF),
        pltpu.VMEM((PLANE - 1, CHUNK, LANES), BF),
        pltpu.VMEM((NZ, CHUNK, LANES), BF),
        pltpu.VMEM((CHUNKS, CHUNK, LANES), BF),
    ]
    for shape in (
        (2, GROUPS, NY - 1),
        (2, 2, STEPS),
        (2, GROUPS),
        (2, GROUPS, NX - 1),
        (NX - 1,),
    ):
        scratch += [dma(shape)] * 2
    scratch += [dma((9,))]
    for count in (1, PLANE - 1, NZ - 1, PLANE - 1, PLANE):
        scratch += [dma((count,))] * 2
    logits, full = pl.pallas_call(
        kernel,
        out_shape=(
            jax.ShapeDtypeStruct((256, 512), BF),
            jax.ShapeDtypeStruct((CHUNKS, CHUNK, LANES), BF),
        ),
        in_specs=[hbm] * 8,
        out_specs=(hbm,) * 2,
        scratch_shapes=scratch,
        compiler_params=pltpu.CompilerParams(
            collective_id=0, has_side_effects=True, vmem_limit_bytes=60 * 1024 * 1024
        ),
        cost_estimate=pl.CostEstimate(
            flops=5_000_000_000, bytes_accessed=5_000_000, transcendentals=4_000_000
        ),
    )(
        tile_values.reshape(ND, SLOTS, TILE, TILE),
        tile_rows[0, 0].T,
        tile_cols[0, 0].T,
        tile_counts.reshape(ND),
        features.reshape(OWN, TILE, TILE),
        weight_in,
        weight_out,
        cotangent,
    )
    return pl.pallas_call(
        unpack,
        out_shape=(
            jax.ShapeDtypeStruct((256, 512), BF),
            jax.ShapeDtypeStruct((TILE, 512), F32),
            jax.ShapeDtypeStruct((512, 512), F32),
        ),
        in_specs=[vmem, vmem],
        out_specs=(vmem, vmem, vmem),
        compiler_params=pltpu.CompilerParams(vmem_limit_bytes=60 * 1024 * 1024),
    )(logits, full)


def solution(mesh):
    placed = (
        P("rep", "dom", None, None, None, None),
        P("rep", "dom", None, None),
        P("rep", "dom", None, None),
        P("rep", "dom", None),
        P(("dom", "rep"), None),
        P(),
        P(),
        P(("dom", "rep"), None),
    )
    return jax.shard_map(
        per_device,
        mesh=mesh,
        in_specs=placed,
        out_specs=(P(("dom", "rep"), None), P(), P()),
        check_vma=False,
    )
```

```python
import jax
import jax.numpy as jnp
from jax import lax
from jax.experimental import pallas as pl
from jax.experimental.pallas import tpu as pltpu
from jax.sharding import PartitionSpec as P

BF = jnp.bfloat16
F32 = jnp.float32

NY, NK, NZ, NX = 4, 2, 8, 4
NR = NY * NK
ND = NZ * NX
SLOTS = 2
TILE = 128
OWN = 2
BLOCKS = NR * OWN
HALF = BLOCKS // NK
MOVED = (6, 7)
STEPS = NZ // 2
GROUPS = NZ
PLANE = NY * NX
LANES = 640
CHUNK = 16
CHUNKS = 512 // CHUNK
SHARE = CHUNKS // NK

OFFSET = [0] + [s * t for t in range(1, STEPS) for s in (-1, 1)] + [STEPS]


def group_of(way, step):
    if step == 0:
        return 0
    if step == STEPS:
        return GROUPS - 1
    return 2 * step - 1 + way


def dot(a, b, ca, cb):
    return lax.dot_general(a, b, (((ca,), (cb,)), ((), ())), preferred_element_type=F32)


def kernel(*refs):
    refs = list(refs)

    def take(n):
        out, refs[:n] = refs[:n], []
        return out

    tiles_h, rows_h, cols_h, counts_h, feat, w_in_h, w_out_h, cot_h = take(8)
    logits_h, full_h = take(2)
    raw = [take(GROUPS), take(GROUPS)]
    picked = take(2)
    sending = take(2)
    tiles, w_in, w_out, cot, rows_s, cols_s, counts_s = take(7)
    far_rows_v, far_rows_s, far_counts_v, far_counts_s = take(4)
    far_tiles, far_spread, far_near, far_acc, far_out, far_in = take(6)
    far_v, far_s, spread, w_in_t, dagg_t, acc1, agg1, acc2, acc3 = take(9)
    agg2_t, logits, red1_out, red1_in, red2_out, red2_in, red3, full = take(8)
    y_s, y_r, b_s, b_r, p_s, p_r, c_s, c_r, col_s, col_r, loc = take(11)
    t_s, t_r, row_s, row_r, count_s, count_r, f_s, f_r = take(8)
    g1_s, g1_r, g2_s, g2_r, g3_s, g3_r, g4_s, g4_r, g5_s, g5_r = take(10)

    r = lax.axis_index("rep")
    d = lax.axis_index("dom")
    y, k = r // NK, r % NK
    z, x = d // NX, d % NX
    left = []

    def send(src, dst, s_sem, r_sem, rr, zz, xx):
        copy = pltpu.make_async_remote_copy(
            src_ref=src,
            dst_ref=dst,
            send_sem=s_sem,
            recv_sem=r_sem,
            device_id=(rr, zz * NX + xx),
            device_id_type=pl.DeviceIdType.MESH,
        )
        copy.start()
        left.append(copy)
        return copy

    def fetch(i, src, dst):
        copy = pltpu.make_async_copy(src, dst, loc.at[i])
        copy.start()
        return copy

    small = [fetch(0, cols_h, cols_s), fetch(1, rows_h, rows_s), fetch(2, counts_h, counts_s)]
    large = [
        fetch(3, tiles_h, tiles),
        fetch(4, w_in_h, w_in),
        fetch(5, w_out_h, w_out),
        fetch(6, cot_h, cot),
    ]

    greet = [(y * NK + 1 - k, z, x)]
    for dx in range(NX):
        for dy in range(NY):
            if dx or dy:
                greet.append((((y + dy) % NY) * NK + k, z, (x + dx) % NX))
    for dz in range(1, NZ):
        greet.append((r, (z + dz) % NZ, x))
    barrier = pltpu.get_barrier_semaphore()
    for rr, zz, xx in greet:
        pl.semaphore_signal(
            barrier, inc=1, device_id=(rr, zz * NX + xx), device_id_type=pl.DeviceIdType.MESH
        )
    pl.semaphore_wait(barrier, len(greet))

    half = pl.ds(HALF * k, HALF)
    at = HALF * k + OWN * y

    def ring(p, own, way, step):
        first, count = (0, OWN) if step < STEPS else (way, 1)
        here = pl.ds(at + first, count)
        src = own if step == 1 else raw[p][group_of(way, step - 1)].at[here]
        return send(
            src,
            raw[p][group_of(way, step)].at[here],
            b_s.at[p, way, step - 1],
            b_r.at[p, way, step - 1],
            r,
            (z + (1, NZ - 1)[way]) % NZ,
            x,
        )

    def gather_y(p, own, g):
        here = pl.ds(at, OWN)
        return [
            send(
                own if g == 0 else raw[p][g].at[here],
                raw[p][g].at[here],
                y_s.at[p, g, dy - 1],
                y_r.at[p, g, dy - 1],
                ((y + dy) % NY) * NK + k,
                z,
                x,
            )
            for dy in range(1, NY)
        ]

    def relay(p, way, i):
        here = pl.ds(HALF * k + OWN * ((y + NY - i) % NY), OWN)
        g = group_of(way, 2)
        return send(
            raw[p][group_of(way, 1)].at[here],
            raw[p][g].at[here],
            y_s.at[p, g, i - 1],
            y_r.at[p, g, i - 1],
            r,
            (z + (1, NZ - 1)[way]) % NZ,
            x,
        )

    def share(p, g):
        return send(
            raw[p][g].at[half],
            raw[p][g].at[half],
            p_s.at[p, g],
            p_r.at[p, g],
            y * NK + 1 - k,
            z,
            x,
        )

    def block(p, g, j):
        return raw[p][g][((j >> 1) & 1) * HALF + (j >> 2) * OWN + (j & 1)]

    def pick(p, g):
        c = ((z + OFFSET[g] + NZ) % NZ) * NX + x
        copies = []
        for dx in (2, 1, 3):
            for s in range(SLOTS):
                sending[p][g, dx - 1, s] = block(p, g, far_s[dx - 1, s, c])
            copies.append(
                send(
                    sending[p].at[g, dx - 1],
                    picked[p].at[g, x],
                    c_s.at[p, g, dx - 1],
                    c_r.at[p, g, dx - 1],
                    r,
                    z,
                    (x + dx) % NX,
                )
            )
        for s in range(SLOTS):
            picked[p][g, x, s] = block(p, g, cols_s[s, c])
        return copies

    def exchange(p, own, keep, ready, early, meanwhile, middle, consume):
        rings = {0: [ring(p, own, 0, 1), ring(p, own, 1, 1)]}
        ys = {0: gather_y(p, own, 0)}
        shares, picks = {}, {}
        keep()

        def do_z(step):
            for copy in rings[step - 1]:
                copy.wait_recv()
            if step < STEPS:
                rings[step] = [ring(p, own, 0, step + 1), ring(p, own, 1, step + 1)]
            for g in sorted({group_of(0, step), group_of(1, step)}):
                if step != 2:
                    ys[g] = gather_y(p, own, g)

        def do_y(g):
            for i, copy in enumerate(ys[g]):
                copy.wait_recv()
                if g in (1, 2):
                    ys.setdefault(g + 2, []).append(relay(p, g - 1, i + 1))
            if g == 0:
                ready()
            shares[g] = share(p, g)

        def do_k(g):
            shares[g].wait_recv()
            picks[g] = pick(p, g)

        def do_c(g):
            for copy in picks[g]:
                copy.wait_recv()
            consume(g, range(NX))

        def do_last(g):
            consume(g, [x])
            picks[g][1].wait_recv()
            picks[g][2].wait_recv()
            consume(g, [(x + 1) % NX, (x + NX - 1) % NX])
            picks[g][0].wait_recv()
            consume(g, [(x + 2) % NX])

        def do_w(g):
            if p == 0 and g in MOVED:
                shares[g].wait_recv()
                moved(g)
            else:
                do_k(g)

        meanwhile()
        do_z(1)
        early()
        do_y(0)
        do_w(0)
        do_z(2)
        do_y(1)
        do_w(1)
        do_z(3)
        do_y(2)
        do_w(2)
        middle()
        do_y(3)
        do_z(4)
        do_w(3)
        do_c(0)
        do_y(5)
        do_w(5)
        do_y(4)
        do_w(4)
        do_c(1)
        do_y(6)
        do_w(6)
        do_c(2)
        do_y(7)
        do_w(7)
        do_c(3)
        do_c(5)
        do_c(4)
        if p == 1:
            do_c(6)
            do_last(7)

    tables = []
    for dx in range(1, NX):
        to = (r, z, (x + NX - dx) % NX)
        i = dx - 1
        tables.append(send(cols_h, far_v.at[i], col_s.at[i], col_r.at[i], *to))
        tables.append(send(rows_h, far_rows_v.at[i], row_s.at[i], row_r.at[i], *to))
        tables.append(send(counts_h, far_counts_v.at[i], count_s.at[i], count_r.at[i], *to))

    def block_of(g):
        return ((z + OFFSET[g] + NZ) % NZ) * NX

    def move_tiles():
        out = []
        for n, g in enumerate(MOVED):
            for dx in (2, 1, 3):
                xx = (x + NX - dx) % NX
                i = dx - 1
                out.append(
                    send(
                        tiles_h.at[block_of(g) + xx],
                        far_tiles.at[n, i],
                        t_s.at[n, i],
                        t_r.at[n, i],
                        r,
                        z,
                        xx,
                    )
                )
        return out

    def early1():
        for copy in tables:
            copy.wait_recv()
        copies = [
            fetch(7, far_v, far_s),
            fetch(9, far_rows_v, far_rows_s),
            fetch(10, far_counts_v, far_counts_s),
        ]
        for copy in copies:
            copy.wait()

    moving = []

    kept = []

    def keep1():
        moving.extend(move_tiles())
        kept.append(fetch(8, feat, raw[0][0].at[pl.ds(at, OWN)]))

    def ready1():
        kept[0].wait()

    def keep2():
        raw[1][0][pl.ds(at, OWN)] = agg1[...]

    def place(into, at, tile, row, live, slot):
        for b in range(OWN):
            into[*at, b * TILE : (b + 1) * TILE, slot * TILE : (slot + 1) * TILE] = jnp.where(
                jnp.logical_and(live, row == b), tile, jnp.zeros_like(tile)
            )

    def meanwhile1():
        for copy in small + large:
            copy.wait()
        for g in range(GROUPS):

            def body(xc, carry, g=g):
                c = block_of(g) + xc
                for t in range(SLOTS):
                    place(spread, (g * NX + xc,), tiles[c, t], rows_s[t, c], t < counts_s[0, c], t)
                return carry

            lax.fori_loop(0, NX, body, 0)
        w_in_t[...] = w_in[...].astype(F32).T.astype(BF)
        dagg_t[...] = dot(w_out[...], cot[...], 1, 1).astype(BF)
        acc1[...] = jnp.zeros_like(acc1)
        acc2[...] = jnp.zeros_like(acc2)
        acc3[...] = jnp.zeros_like(acc3)

    def consume1(g, pieces):
        total = acc1[...]
        for xc in pieces:
            near = picked[0][g, xc].reshape(SLOTS * TILE, TILE)
            total = total + dot(spread[g * NX + xc], near, 1, 0)
        acc1[...] = total

    def middle1():
        for copy in moving:
            copy.wait_recv()
        for n, g in enumerate(MOVED):
            c = block_of(g) + x
            for i in range(NX - 1):
                for t in range(SLOTS):
                    live = t < far_counts_s[i, 0, c]
                    place(far_spread, (n, i), far_tiles[n, i, t], far_rows_s[i, t, c], live, t)

    far_copies = []

    def moved(g):
        n = MOVED.index(g)
        c = block_of(g) + x
        for i in range(NX - 1):
            for t in range(SLOTS):
                far_near[i, t] = block(0, g, far_s[i, t, c])
            term = dot(far_spread[n, i], far_near[i].reshape(SLOTS * TILE, TILE), 1, 0)
            far_acc[i] = term if n == 0 else far_acc[i] + term
        if n == len(MOVED) - 1:
            far_out[...] = far_acc[...].astype(BF)
            for dx in (2, 1, 3):
                i = dx - 1
                far_copies.append(
                    send(far_out.at[i], far_in.at[i], f_s.at[i], f_r.at[i], r, z, (x + dx) % NX)
                )
        for t in range(SLOTS):
            far_near[NX - 1, t] = block(0, g, cols_s[t, c])
        near = far_near[NX - 1].reshape(SLOTS * TILE, TILE)
        acc1[...] += dot(spread[g * NX + x], near, 1, 0)

    def nothing(g=None):
        pass

    exchange(0, feat, keep1, ready1, early1, meanwhile1, middle1, consume1)
    total = acc1[...]
    for i, copy in enumerate(far_copies):
        copy.wait_recv()
        total = total + far_in[(1, 0, 2)[i]].astype(F32)
    agg1[...] = total.astype(BF).reshape(OWN, TILE, TILE)

    def consume2(g, pieces):
        for xc in pieces:
            near = picked[1][g, xc].reshape(SLOTS * TILE, TILE)
            tile = spread[g * NX + xc]
            z1 = dot(w_in_t[...], near, 1, 1)
            sig = 0.5 + 0.5 * jnp.tanh(0.5 * z1)
            hidden = z1 * sig
            slope = sig + hidden * (1.0 - sig)
            acc2[...] += dot(hidden.astype(BF), tile, 1, 1)
            dz = (dot(dagg_t[...], tile, 1, 0) * slope).astype(BF)
            acc3[...] += dot(dz, near, 1, 0)

    exchange(1, agg1, keep2, nothing, nothing, nothing, nothing, consume2)

    agg2_t[...] = acc2[...].astype(BF)

    def term(core):
        rows = pl.ds(256 * core, 256)
        return (
            dot(agg2_t[rows], cot[...], 1, 0).reshape(SHARE, CHUNK, 512),
            acc3[rows].reshape(SHARE, CHUNK, TILE),
        )

    out, back = term(1 - k)
    red1_out[:, :, 0:512] = out.astype(BF)
    red1_out[:, :, 512:LANES] = back.astype(BF)
    copy = send(red1_out, red1_in, g1_s.at[0], g1_r.at[0], y * NK + 1 - k, z, x)
    out, back = term(k)
    copy.wait_recv()
    red2_out[:, :, 0:512] = (out + red1_in[:, :, 0:512].astype(F32)).astype(BF)
    red2_out[:, :, 512:LANES] = (back + red1_in[:, :, 512:LANES].astype(F32)).astype(BF)
    me = y * NX + x
    plane = [(dy, dx) for dy in range(NY) for dx in range(NX) if dy or dx]
    plane.sort(key=lambda step: -min(step[0], NY - step[0]) - min(step[1], NX - step[1]))
    copies = []
    for i, (dy, dx) in enumerate(plane):
        yy, xx = (y + dy) % NY, (x + dx) % NX
        copies.append(
            send(red2_out.at[yy * NX + xx], red2_in.at[i], g2_s.at[i], g2_r.at[i], yy * NK + k, z, xx)
        )
    logits[...] = dot(agg2_t[...], w_out[...], 0, 0).astype(BF)
    done = fetch(0, logits, logits_h)
    total = red2_out[me].astype(F32)
    for i in range(PLANE - 2, -1, -1):
        copies[i].wait_recv()
        total = total + red2_in[i].astype(F32)
    red3[z] = total.astype(BF)
    copies = [
        send(red3.at[z], red3.at[z], g3_s.at[i - 1], g3_r.at[i - 1], r, (z + i) % NZ, x)
        for i in (4, 3, 5, 2, 6, 1, 7)
    ]
    for copy in copies:
        copy.wait_recv()
    total = red3[0].astype(F32)
    for i in range(1, NZ):
        total = total + red3[i].astype(F32)

    def to_core(i, chunk):
        return send(chunk, chunk, g5_s.at[i], g5_r.at[i], y * NK + 1 - k, z, x)

    full[SHARE * k + me] = total.astype(BF)
    chunk = full.at[SHARE * k + me]
    copies = []
    for i, (dy, dx) in enumerate(plane):
        yy, xx = (y + dy) % NY, (x + dx) % NX
        copies.append(send(chunk, chunk, g4_s.at[i], g4_r.at[i], yy * NK + k, z, xx))
    others = [to_core(PLANE - 1, chunk)]
    for i in range(PLANE - 2, -1, -1):
        copies[i].wait_recv()
        dy, dx = plane[i]
        came = ((y + NY - dy) % NY) * NX + (x + NX - dx) % NX
        others.append(to_core(i, full.at[SHARE * k + came]))
    for copy in others:
        copy.wait_recv()
    last = fetch(1, full, full_h)
    for copy in left:
        copy.wait_send()
    done.wait()
    last.wait()


def unpack(logits_in, full, logits, grad_in, grad_out):
    logits[...] = logits_in[...]
    grad_out[...] = full[:, :, 0:512].astype(F32).reshape(512, 512)
    grad_in[...] = full[:, :, 512:LANES].astype(F32).reshape(512, TILE).T


def per_device(
    tile_values, tile_rows, tile_cols, tile_counts, features, weight_in, weight_out, cotangent
):
    vmem = pl.BlockSpec(memory_space=pltpu.VMEM)
    hbm = pl.BlockSpec(memory_space=pltpu.HBM)
    block = pltpu.VMEM((BLOCKS, TILE, TILE), BF)
    dma = pltpu.SemaphoreType.DMA
    scratch = [block] * (2 * GROUPS)
    scratch += [pltpu.VMEM((GROUPS, NX, SLOTS, TILE, TILE), BF)] * 2
    scratch += [pltpu.VMEM((GROUPS, NX - 1, SLOTS, TILE, TILE), BF)] * 2
    scratch += [
        pltpu.VMEM((ND, SLOTS, TILE, TILE), BF),
        pltpu.VMEM((TILE, 512), BF),
        pltpu.VMEM((512, 512), BF),
        pltpu.VMEM((256, 512), BF),
        pltpu.SMEM((SLOTS, ND), jnp.int32),
        pltpu.SMEM((SLOTS, ND), jnp.int32),
        pltpu.SMEM((1, ND), jnp.int32),
        pltpu.VMEM((NX - 1, SLOTS, ND), jnp.int32),
        pltpu.SMEM((NX - 1, SLOTS, ND), jnp.int32),
        pltpu.VMEM((NX - 1, 1, ND), jnp.int32),
        pltpu.SMEM((NX - 1, 1, ND), jnp.int32),
        pltpu.VMEM((len(MOVED), NX - 1, SLOTS, TILE, TILE), BF),
        pltpu.VMEM((len(MOVED), NX - 1, 256, 256), BF),
        pltpu.VMEM((NX, SLOTS, TILE, TILE), BF),
        pltpu.VMEM((NX - 1, 256, TILE), F32),
        pltpu.VMEM((NX - 1, 256, TILE), BF),
        pltpu.VMEM((NX - 1, 256, TILE), BF),
        pltpu.VMEM((NX - 1, SLOTS, ND), jnp.int32),
        pltpu.SMEM((NX - 1, SLOTS, ND), jnp.int32),
        pltpu.VMEM((ND, 256, 256), BF),
        pltpu.VMEM((512, TILE), BF),
        pltpu.VMEM((512, 256), BF),
        pltpu.VMEM((256, TILE), F32),
        pltpu.VMEM((OWN, TILE, TILE), BF),
        pltpu.VMEM((512, 256), F32),
        pltpu.VMEM((512, TILE), F32),
        pltpu.VMEM((512, 256), BF),
        pltpu.VMEM((256, 512), BF),
        pltpu.VMEM((SHARE, CHUNK, LANES), BF),
        pltpu.VMEM((SHARE, CHUNK, LANES), BF),
        pltpu.VMEM((SHARE, CHUNK, LANES), BF),
        pltpu.VMEM((PLANE - 1, CHUNK, LANES), BF),
        pltpu.VMEM((NZ, CHUNK, LANES), BF),
        pltpu.VMEM((CHUNKS, CHUNK, LANES), BF),
    ]
    for shape in (
        (2, GROUPS, NY - 1),
        (2, 2, STEPS),
        (2, GROUPS),
        (2, GROUPS, NX - 1),
        (NX - 1,),
    ):
        scratch += [dma(shape)] * 2
    scratch += [dma((11,))]
    for shape in ((len(MOVED), NX - 1), (NX - 1,), (NX - 1,), (NX - 1,)):
        scratch += [dma(shape)] * 2
    for count in (1, PLANE - 1, NZ - 1, PLANE - 1, PLANE):
        scratch += [dma((count,))] * 2
    logits, full = pl.pallas_call(
        kernel,
        out_shape=(
            jax.ShapeDtypeStruct((256, 512), BF),
            jax.ShapeDtypeStruct((CHUNKS, CHUNK, LANES), BF),
        ),
        in_specs=[hbm] * 8,
        out_specs=(hbm,) * 2,
        scratch_shapes=scratch,
        compiler_params=pltpu.CompilerParams(
            collective_id=0, has_side_effects=True, vmem_limit_bytes=60 * 1024 * 1024
        ),
        cost_estimate=pl.CostEstimate(
            flops=5_000_000_000, bytes_accessed=5_000_000, transcendentals=4_000_000
        ),
    )(
        tile_values.reshape(ND, SLOTS, TILE, TILE),
        tile_rows[0, 0].T,
        tile_cols[0, 0].T,
        tile_counts[0],
        features.reshape(OWN, TILE, TILE),
        weight_in,
        weight_out,
        cotangent,
    )
    return pl.pallas_call(
        unpack,
        out_shape=(
            jax.ShapeDtypeStruct((256, 512), BF),
            jax.ShapeDtypeStruct((TILE, 512), F32),
            jax.ShapeDtypeStruct((512, 512), F32),
        ),
        in_specs=[vmem, vmem],
        out_specs=(vmem, vmem, vmem),
        compiler_params=pltpu.CompilerParams(vmem_limit_bytes=60 * 1024 * 1024),
    )(logits, full)


def solution(mesh):
    placed = (
        P("rep", "dom", None, None, None, None),
        P("rep", "dom", None, None),
        P("rep", "dom", None, None),
        P("rep", "dom", None),
        P(("dom", "rep"), None),
        P(),
        P(),
        P(("dom", "rep"), None),
    )
    return jax.shard_map(
        per_device,
        mesh=mesh,
        in_specs=placed,
        out_specs=(P(("dom", "rep"), None), P(), P()),
        check_vma=False,
    )
```

```python
import jax
import jax.numpy as jnp
from jax import lax
from jax.experimental import pallas as pl
from jax.experimental.pallas import tpu as pltpu
from jax.sharding import PartitionSpec as P

BF = jnp.bfloat16
F32 = jnp.float32

NY, NK, NZ, NX = 4, 2, 8, 4
NR = NY * NK
ND = NZ * NX
SLOTS = 2
TILE = 128
OWN = 2
BLOCKS = NR * OWN
HALF = BLOCKS // NK
MOVED = (6, 7)
STEPS = NZ // 2
GROUPS = NZ
PLANE = NY * NX
LANES = 640
WIDE = 512
CHUNK = 16
CHUNKS = 512 // CHUNK
SHARE = CHUNKS // NK

OFFSET = [0] + [s * t for t in range(1, STEPS) for s in (-1, 1)] + [STEPS]


def group_of(way, step):
    if step == 0:
        return 0
    if step == STEPS:
        return GROUPS - 1
    return 2 * step - 1 + way


def dot(a, b, ca, cb):
    return lax.dot_general(a, b, (((ca,), (cb,)), ((), ())), preferred_element_type=F32)


def kernel(*refs):
    refs = list(refs)

    def take(n):
        out, refs[:n] = refs[:n], []
        return out

    tiles_h, rows_h, cols_h, counts_h, feat, w_in_h, w_out_h, cot_h = take(8)
    logits_h, full_h, small_h = take(3)
    raw = [take(GROUPS), take(GROUPS)]
    picked = take(2)
    sending = take(2)
    tiles, w_in, w_out, cot, rows_s, cols_s, counts_s = take(7)
    far_rows_v, far_rows_s, far_counts_v, far_counts_s = take(4)
    far_tiles, far_spread, far_near, far_acc, far_out, far_in = take(6)
    far_v, far_s, spread, w_in_t, dagg_t, acc1, agg1, acc2, acc3 = take(9)
    agg2_t, logits, red1_out, red1_in, red2_out, red2_in, red3, full = take(8)
    low_out, low_in, low_sum, low_full = take(4)
    sent, y_r, piece_r, b_r, p_r, c_r, last_r, col_s, col_r, row_s, row_r = take(11)
    count_s, count_r, t_r, f_r, ar_r, g4_r, loc = take(7)

    r = lax.axis_index("rep")
    d = lax.axis_index("dom")
    y, k = r // NK, r % NK
    z, x = d // NX, d % NX

    def copy_to(src, dst, s_sem, r_sem, rr, zz, xx):
        copy = pltpu.make_async_remote_copy(
            src_ref=src,
            dst_ref=dst,
            send_sem=s_sem,
            recv_sem=r_sem,
            device_id=(rr, zz * NX + xx),
            device_id_type=pl.DeviceIdType.MESH,
        )
        copy.start()
        return copy

    def wait_bytes(like, sem):
        pltpu.make_async_copy(like, like, sem).wait()

    def send(src, dst, kind, r_sem, rr, zz, xx):
        return copy_to(src, dst, sent.at[kind], r_sem, rr, zz, xx)

    def fetch(i, src, dst):
        copy = pltpu.make_async_copy(src, dst, loc.at[i])
        copy.start()
        return copy

    small = [fetch(0, cols_h, cols_s), fetch(1, rows_h, rows_s), fetch(2, counts_h, counts_s)]
    large = [
        fetch(3, tiles_h, tiles),
        fetch(4, w_in_h, w_in),
        fetch(5, w_out_h, w_out),
        fetch(6, cot_h, cot),
    ]

    greet = [(y * NK + 1 - k, z, x)]
    greet += [(((y + dy) % NY) * NK + k, z, x) for dy in range(1, NY)]
    greet += [(r, z, (x + dx) % NX) for dx in range(1, NX)]
    greet += [(r, (z + dz) % NZ, x) for dz in (1, NZ - 1)]
    barrier = pltpu.get_barrier_semaphore()
    for rr, zz, xx in greet:
        pl.semaphore_signal(
            barrier, inc=1, device_id=(rr, zz * NX + xx), device_id_type=pl.DeviceIdType.MESH
        )
    pl.semaphore_wait(barrier, len(greet))

    half = pl.ds(HALF * k, HALF)
    at = HALF * k + OWN * y

    def ring(p, own, way, step):
        first, count = (0, OWN) if step < STEPS else (way, 1)
        here = pl.ds(at + first, count)
        src = own if step == 1 else raw[p][group_of(way, step - 1)].at[here]
        return send(
            src,
            raw[p][group_of(way, step)].at[here],
            2 + p,
            b_r.at[p, step - 1],
            r,
            (z + (1, NZ - 1)[way]) % NZ,
            x,
        )

    def gather_y(p, own, g):
        here = pl.ds(at, OWN)
        return [
            send(
                own if g == 0 else raw[p][g].at[here],
                raw[p][g].at[here],
                p,
                piece_r.at[p, g - 1, dy - 1] if g in (1, 2) else y_r.at[p, g],
                ((y + dy) % NY) * NK + k,
                z,
                x,
            )
            for dy in range(1, NY)
        ]

    def relay(p, way, i):
        here = pl.ds(HALF * k + OWN * ((y + NY - i) % NY), OWN)
        g = group_of(way, 2)
        return send(
            raw[p][group_of(way, 1)].at[here],
            raw[p][g].at[here],
            p,
            y_r.at[p, g],
            r,
            (z + (1, NZ - 1)[way]) % NZ,
            x,
        )

    def share(p, g):
        return send(
            raw[p][g].at[half],
            raw[p][g].at[half],
            4 + p,
            p_r.at[p, g],
            y * NK + 1 - k,
            z,
            x,
        )

    def block(p, g, j):
        return raw[p][g][((j >> 1) & 1) * HALF + (j >> 2) * OWN + (j & 1)]

    def pick(p, g):
        c = ((z + OFFSET[g] + NZ) % NZ) * NX + x
        copies = []
        for dx in (2, 1, 3):
            for s in range(SLOTS):
                sending[p][g, dx - 1, s] = block(p, g, far_s[dx - 1, s, c])
            copies.append(
                send(
                    sending[p].at[g, dx - 1],
                    picked[p].at[g, x],
                    6 + p,
                    last_r.at[dx - 1] if p == 1 and g == GROUPS - 1 else c_r.at[p, g],
                    r,
                    z,
                    (x + dx) % NX,
                )
            )
        for s in range(SLOTS):
            picked[p][g, x, s] = block(p, g, cols_s[s, c])
        return copies

    def exchange(p, own, keep, ready, early, meanwhile, middle, consume):
        rings = {0: [ring(p, own, 0, 1), ring(p, own, 1, 1)]}
        ys = {0: gather_y(p, own, 0)}
        shares, picks = {}, {}
        keep()

        def do_z(step):
            wait_bytes(raw[p][0].at[pl.ds(0, 2 * OWN if step < STEPS else OWN)], b_r.at[p, step - 1])
            if step < STEPS:
                rings[step] = [ring(p, own, 0, step + 1), ring(p, own, 1, step + 1)]
            for g in sorted({group_of(0, step), group_of(1, step)}):
                if step != 2:
                    ys[g] = gather_y(p, own, g)

        def do_y(g):
            if g in (1, 2):
                for i, copy in enumerate(ys[g]):
                    copy.wait_recv()
                    relay(p, g - 1, i + 1)
            else:
                wait_bytes(raw[p][g].at[pl.ds(0, (NY - 1) * OWN)], y_r.at[p, g])
            if g == 0:
                ready()
            shares[g] = share(p, g)

        def do_k(g):
            shares[g].wait_recv()
            picks[g] = pick(p, g)

        def do_c(g):
            wait_bytes(sending[p].at[g], c_r.at[p, g])
            consume(g, range(NX))

        def do_last(g):
            consume(g, [x])
            picks[g][1].wait_recv()
            picks[g][2].wait_recv()
            consume(g, [(x + 1) % NX, (x + NX - 1) % NX])
            picks[g][0].wait_recv()
            consume(g, [(x + 2) % NX])

        def do_w(g):
            if p == 0 and g in MOVED:
                shares[g].wait_recv()
                moved(g)
            else:
                do_k(g)

        meanwhile()
        do_z(1)
        early()
        do_y(0)
        do_w(0)
        do_z(2)
        do_y(1)
        do_w(1)
        do_z(3)
        do_y(2)
        do_w(2)
        middle()
        do_y(3)
        do_z(4)
        do_w(3)
        do_c(0)
        do_y(5)
        do_w(5)
        do_y(4)
        do_w(4)
        do_c(1)
        do_y(6)
        do_w(6)
        do_c(2)
        do_y(7)
        do_w(7)
        do_c(3)
        do_c(5)
        do_c(4)
        if p == 1:
            do_c(6)
            do_last(7)

    tables = []
    for dx in range(1, NX):
        to = (r, z, (x + NX - dx) % NX)
        i = dx - 1
        tables.append(copy_to(cols_h, far_v.at[i], col_s.at[i], col_r.at[i], *to))
        tables.append(copy_to(rows_h, far_rows_v.at[i], row_s.at[i], row_r.at[i], *to))
        tables.append(copy_to(counts_h, far_counts_v.at[i], count_s.at[i], count_r.at[i], *to))

    def block_of(g):
        return ((z + OFFSET[g] + NZ) % NZ) * NX

    def move_tiles():
        for n, g in enumerate(MOVED):
            for dx in (2, 1, 3):
                xx = (x + NX - dx) % NX
                tile = tiles_h.at[block_of(g) + xx]
                send(tile, far_tiles.at[n, dx - 1], 8, t_r.at[0], r, z, xx)

    def early1():
        for copy in tables:
            copy.wait_recv()
        copies = [
            fetch(7, far_v, far_s),
            fetch(9, far_rows_v, far_rows_s),
            fetch(10, far_counts_v, far_counts_s),
        ]
        for copy in copies:
            copy.wait()

    kept = []

    def keep1():
        move_tiles()
        kept.append(fetch(8, feat, raw[0][0].at[pl.ds(at, OWN)]))

    def ready1():
        kept[0].wait()

    def keep2():
        raw[1][0][pl.ds(at, OWN)] = agg1[...]

    def place(into, at, tile, row, live, slot):
        for b in range(OWN):
            into[*at, b * TILE : (b + 1) * TILE, slot * TILE : (slot + 1) * TILE] = jnp.where(
                jnp.logical_and(live, row == b), tile, jnp.zeros_like(tile)
            )

    def meanwhile1():
        for copy in small + large:
            copy.wait()
        for g in range(GROUPS):

            def body(xc, carry, g=g):
                c = block_of(g) + xc
                for t in range(SLOTS):
                    place(spread, (g * NX + xc,), tiles[c, t], rows_s[t, c], t < counts_s[0, c], t)
                return carry

            lax.fori_loop(0, NX, body, 0)
        w_in_t[...] = w_in[...].astype(F32).T.astype(BF)
        dagg_t[...] = dot(w_out[...], cot[...], 1, 1).astype(BF)
        acc1[...] = jnp.zeros_like(acc1)
        acc2[...] = jnp.zeros_like(acc2)
        acc3[...] = jnp.zeros_like(acc3)

    def consume1(g, pieces):
        total = acc1[...]
        for xc in pieces:
            near = picked[0][g, xc].reshape(SLOTS * TILE, TILE)
            total = total + dot(spread[g * NX + xc], near, 1, 0)
        acc1[...] = total

    def middle1():
        wait_bytes(far_tiles, t_r.at[0])
        for n, g in enumerate(MOVED):
            c = block_of(g) + x
            for i in range(NX - 1):
                for t in range(SLOTS):
                    live = t < far_counts_s[i, 0, c]
                    place(far_spread, (n, i), far_tiles[n, i, t], far_rows_s[i, t, c], live, t)

    def moved(g):
        n = MOVED.index(g)
        c = block_of(g) + x
        for i in range(NX - 1):
            for t in range(SLOTS):
                far_near[i, t] = block(0, g, far_s[i, t, c])
            term = dot(far_spread[n, i], far_near[i].reshape(SLOTS * TILE, TILE), 1, 0)
            far_acc[i] = term if n == 0 else far_acc[i] + term
        if n == len(MOVED) - 1:
            far_out[...] = far_acc[...].astype(BF)
            for dx in (2, 1, 3):
                i = dx - 1
                send(far_out.at[i], far_in.at[i], 9, f_r.at[0], r, z, (x + dx) % NX)
        for t in range(SLOTS):
            far_near[NX - 1, t] = block(0, g, cols_s[t, c])
        near = far_near[NX - 1].reshape(SLOTS * TILE, TILE)
        acc1[...] += dot(spread[g * NX + x], near, 1, 0)

    def nothing(g=None):
        pass

    exchange(0, feat, keep1, ready1, early1, meanwhile1, middle1, consume1)
    total = acc1[...]
    wait_bytes(far_in, f_r.at[0])
    for i in range(NX - 1):
        total = total + far_in[i].astype(F32)
    agg1[...] = total.astype(BF).reshape(OWN, TILE, TILE)

    def consume2(g, pieces):
        for xc in pieces:
            near = picked[1][g, xc].reshape(SLOTS * TILE, TILE)
            tile = spread[g * NX + xc]
            z1 = dot(w_in_t[...], near, 1, 1)
            sig = 0.5 + 0.5 * jnp.tanh(0.5 * z1)
            hidden = z1 * sig
            slope = sig + hidden * (1.0 - sig)
            acc2[...] += dot(hidden.astype(BF), tile, 1, 1)
            dz = (dot(dagg_t[...], tile, 1, 0) * slope).astype(BF)
            acc3[...] += dot(dz, near, 1, 0)

    exchange(1, agg1, keep2, nothing, nothing, nothing, nothing, consume2)

    agg2_t[...] = acc2[...].astype(BF)

    def term(core):
        rows = pl.ds(256 * core, 256)
        return (
            dot(agg2_t[rows], cot[...], 1, 0).reshape(SHARE, CHUNK, 512),
            acc3[rows].reshape(SHARE, CHUNK, TILE),
        )

    out, back = term(1 - k)
    red1_out[:, :, 0:512] = out.astype(BF)
    red1_out[:, :, 512:LANES] = back.astype(BF)
    copy = send(red1_out, red1_in, 10, ar_r.at[0], y * NK + 1 - k, z, x)
    out, back = term(k)
    copy.wait_recv()
    red2_out[...] = (out + red1_in[:, :, 0:WIDE].astype(F32)).astype(BF)
    low_out[...] = (back + red1_in[:, :, WIDE:LANES].astype(F32)).astype(BF)

    me = y * NX + x
    plane = [(dy, dx) for dy in range(NY) for dx in range(NX) if dy or dx]
    plane.sort(key=lambda step: -min(step[0], NY - step[0]) - min(step[1], NX - step[1]))
    there = [((y + dy) % NY, (x + dx) % NX) for dy, dx in plane]
    along = [(z + i) % NZ for i in (4, 3, 5, 2, 6, 1, 7)]
    for i, (yy, xx) in enumerate(there):
        send(red2_out.at[yy * NX + xx], red2_in.at[i], 11, ar_r.at[1], yy * NK + k, z, xx)
    for i, zz in enumerate(along):
        send(low_out.at[pl.ds(2 * zz, 2)], low_in.at[i], 12, ar_r.at[2], r, zz, x)
    logits[...] = dot(agg2_t[...], w_out[...], 0, 0).astype(BF)
    done = fetch(0, logits, logits_h)

    wait_bytes(low_in, ar_r.at[2])
    total = low_out[pl.ds(2 * z, 2)].astype(F32)
    for i in range(NZ - 1):
        total = total + low_in[i].astype(F32)
    low_sum[me] = total.astype(BF)
    for yy, xx in there:
        send(low_sum.at[me], low_sum.at[me], 13, ar_r.at[3], yy * NK + k, z, xx)

    wait_bytes(red2_in, ar_r.at[1])
    total = red2_out[me].astype(F32)
    for i in range(PLANE - 1):
        total = total + red2_in[i].astype(F32)
    red3[z] = total.astype(BF)
    for zz in along:
        send(red3.at[z], red3.at[z], 14, ar_r.at[4], r, zz, x)

    wait_bytes(low_sum.at[pl.ds(0, PLANE - 1)], ar_r.at[3])
    total = low_sum[0].astype(F32)
    for i in range(1, PLANE):
        total = total + low_sum[i].astype(F32)
    here = pl.ds(SHARE * k + 2 * z, 2)
    low_full[here] = total.astype(BF)
    for zz in along:
        send(low_full.at[here], low_full.at[here], 15, ar_r.at[5], r, zz, x)

    wait_bytes(red3.at[pl.ds(0, NZ - 1)], ar_r.at[4])
    total = red3[0].astype(F32)
    for i in range(1, NZ):
        total = total + red3[i].astype(F32)
    full[SHARE * k + me] = total.astype(BF)
    chunk = full.at[SHARE * k + me]
    copies = [
        send(chunk, chunk, 16, g4_r.at[i], yy * NK + k, z, xx) for i, (yy, xx) in enumerate(there)
    ]

    def to_core(chunk, n):
        return send(chunk, chunk, 17 + n, ar_r.at[6 + n], y * NK + 1 - k, z, x)

    to_core(chunk, 0)
    wait_bytes(low_full.at[pl.ds(0, 2 * (NZ - 1))], ar_r.at[5])
    mine = pl.ds(SHARE * k, SHARE)
    to_core(low_full.at[mine], 1)
    for i in range(PLANE - 2, -1, -1):
        copies[i].wait_recv()
        dy, dx = plane[i]
        came = ((y + NY - dy) % NY) * NX + (x + NX - dx) % NX
        to_core(full.at[SHARE * k + came], 0)
    half_full = full.at[mine]
    half_low = low_full.at[mine]
    wait_bytes(half_low, ar_r.at[7])
    last = [fetch(2, low_full, small_h)]
    wait_bytes(half_full, ar_r.at[6])
    last.append(fetch(1, full, full_h))

    for copy in tables:
        copy.wait_send()
    for p in range(2):
        wait_bytes(sending[p], sent.at[p])
        wait_bytes(raw[p][0].at[pl.ds(0, 2 * OWN * (STEPS - 1) + OWN)], sent.at[2 + p])
        wait_bytes(picked[p], sent.at[4 + p])
    wait_bytes(sending[0].at[pl.ds(0, GROUPS - len(MOVED))], sent.at[6])
    wait_bytes(sending[1], sent.at[7])
    wait_bytes(far_tiles, sent.at[8])
    wait_bytes(far_out, sent.at[9])
    wait_bytes(red1_out, sent.at[10])
    wait_bytes(red2_in, sent.at[11])
    wait_bytes(low_in, sent.at[12])
    wait_bytes(low_sum.at[pl.ds(0, PLANE - 1)], sent.at[13])
    wait_bytes(red3.at[pl.ds(0, NZ - 1)], sent.at[14])
    wait_bytes(low_full.at[pl.ds(0, 2 * (NZ - 1))], sent.at[15])
    wait_bytes(red2_in, sent.at[16])
    wait_bytes(half_full, sent.at[17])
    wait_bytes(half_low, sent.at[18])
    done.wait()
    for copy in last:
        copy.wait()


def unpack(logits_in, full, low, logits, grad_in, grad_out):
    logits[...] = logits_in[...]
    grad_out[...] = full[...].astype(F32).reshape(512, WIDE)
    grad_in[...] = low[...].astype(F32).reshape(512, TILE).T


def per_device(
    tile_values, tile_rows, tile_cols, tile_counts, features, weight_in, weight_out, cotangent
):
    vmem = pl.BlockSpec(memory_space=pltpu.VMEM)
    hbm = pl.BlockSpec(memory_space=pltpu.HBM)
    block = pltpu.VMEM((BLOCKS, TILE, TILE), BF)
    dma = pltpu.SemaphoreType.DMA
    scratch = [block] * (2 * GROUPS)
    scratch += [pltpu.VMEM((GROUPS, NX, SLOTS, TILE, TILE), BF)] * 2
    scratch += [pltpu.VMEM((GROUPS, NX - 1, SLOTS, TILE, TILE), BF)] * 2
    scratch += [
        pltpu.VMEM((ND, SLOTS, TILE, TILE), BF),
        pltpu.VMEM((TILE, 512), BF),
        pltpu.VMEM((512, 512), BF),
        pltpu.VMEM((256, 512), BF),
        pltpu.SMEM((SLOTS, ND), jnp.int32),
        pltpu.SMEM((SLOTS, ND), jnp.int32),
        pltpu.SMEM((1, ND), jnp.int32),
        pltpu.VMEM((NX - 1, SLOTS, ND), jnp.int32),
        pltpu.SMEM((NX - 1, SLOTS, ND), jnp.int32),
        pltpu.VMEM((NX - 1, 1, ND), jnp.int32),
        pltpu.SMEM((NX - 1, 1, ND), jnp.int32),
        pltpu.VMEM((len(MOVED), NX - 1, SLOTS, TILE, TILE), BF),
        pltpu.VMEM((len(MOVED), NX - 1, 256, 256), BF),
        pltpu.VMEM((NX, SLOTS, TILE, TILE), BF),
        pltpu.VMEM((NX - 1, 256, TILE), F32),
        pltpu.VMEM((NX - 1, 256, TILE), BF),
        pltpu.VMEM((NX - 1, 256, TILE), BF),
        pltpu.VMEM((NX - 1, SLOTS, ND), jnp.int32),
        pltpu.SMEM((NX - 1, SLOTS, ND), jnp.int32),
        pltpu.VMEM((ND, 256, 256), BF),
        pltpu.VMEM((512, TILE), BF),
        pltpu.VMEM((512, 256), BF),
        pltpu.VMEM((256, TILE), F32),
        pltpu.VMEM((OWN, TILE, TILE), BF),
        pltpu.VMEM((512, 256), F32),
        pltpu.VMEM((512, TILE), F32),
        pltpu.VMEM((512, 256), BF),
        pltpu.VMEM((256, 512), BF),
        pltpu.VMEM((SHARE, CHUNK, LANES), BF),
        pltpu.VMEM((SHARE, CHUNK, LANES), BF),
        pltpu.VMEM((SHARE, CHUNK, WIDE), BF),
        pltpu.VMEM((PLANE - 1, CHUNK, WIDE), BF),
        pltpu.VMEM((NZ, CHUNK, WIDE), BF),
        pltpu.VMEM((CHUNKS, CHUNK, WIDE), BF),
        pltpu.VMEM((SHARE, CHUNK, TILE), BF),
        pltpu.VMEM((NZ - 1, 2, CHUNK, TILE), BF),
        pltpu.VMEM((PLANE, 2, CHUNK, TILE), BF),
        pltpu.VMEM((CHUNKS, CHUNK, TILE), BF),
    ]
    for shape in (
        (19,),
        (2, GROUPS),
        (2, 2, NY - 1),
        (2, STEPS),
        (2, GROUPS),
        (2, GROUPS),
        (NX - 1,),
    ):
        scratch.append(dma(shape))
    scratch += [dma((NX - 1,))] * 6
    scratch += [dma((1,)), dma((1,)), dma((8,)), dma((PLANE - 1,)), dma((11,))]
    logits, full, low = pl.pallas_call(
        kernel,
        out_shape=(
            jax.ShapeDtypeStruct((256, 512), BF),
            jax.ShapeDtypeStruct((CHUNKS, CHUNK, WIDE), BF),
            jax.ShapeDtypeStruct((CHUNKS, CHUNK, TILE), BF),
        ),
        in_specs=[hbm] * 8,
        out_specs=(hbm,) * 3,
        scratch_shapes=scratch,
        compiler_params=pltpu.CompilerParams(
            collective_id=0, has_side_effects=True, vmem_limit_bytes=60 * 1024 * 1024
        ),
        cost_estimate=pl.CostEstimate(
            flops=5_000_000_000, bytes_accessed=5_000_000, transcendentals=4_000_000
        ),
    )(
        tile_values.reshape(ND, SLOTS, TILE, TILE),
        tile_rows[0, 0].T,
        tile_cols[0, 0].T,
        tile_counts[0],
        features.reshape(OWN, TILE, TILE),
        weight_in,
        weight_out,
        cotangent,
    )
    return pl.pallas_call(
        unpack,
        out_shape=(
            jax.ShapeDtypeStruct((256, 512), BF),
            jax.ShapeDtypeStruct((TILE, 512), F32),
            jax.ShapeDtypeStruct((512, 512), F32),
        ),
        in_specs=[vmem] * 3,
        out_specs=(vmem, vmem, vmem),
        compiler_params=pltpu.CompilerParams(vmem_limit_bytes=60 * 1024 * 1024),
    )(logits, full, low)


def solution(mesh):
    placed = (
        P("rep", "dom", None, None, None, None),
        P("rep", "dom", None, None),
        P("rep", "dom", None, None),
        P("rep", "dom", None),
        P(("dom", "rep"), None),
        P(),
        P(),
        P(("dom", "rep"), None),
    )
    return jax.shard_map(
        per_device,
        mesh=mesh,
        in_specs=placed,
        out_specs=(P(("dom", "rep"), None), P(), P()),
        check_vma=False,
    )
```

```python
import jax
import jax.numpy as jnp
from jax import lax
from jax.experimental import pallas as pl
from jax.experimental.pallas import tpu as pltpu
from jax.sharding import PartitionSpec as P

BF = jnp.bfloat16
F32 = jnp.float32

NY, NK, NZ, NX = 4, 2, 8, 4
NR = NY * NK
ND = NZ * NX
SLOTS = 2
TILE = 128
OWN = 2
BLOCKS = NR * OWN
HALF = BLOCKS // NK
EARLY = (0, 1, 2)
LAST = 5
MOVED = (6, 7, LAST)
STEPS = NZ // 2
GROUPS = NZ
PLANE = NY * NX
FAR_FIRST = (2, 1, 3)
LANES = 640
WIDE = 512
CHUNK = 16
CHUNKS = 512 // CHUNK
SHARE = CHUNKS // NK

OFFSET = [0] + [s * t for t in range(1, STEPS) for s in (-1, 1)] + [STEPS]


def group_of(way, step):
    if step == 0:
        return 0
    if step == STEPS:
        return GROUPS - 1
    return 2 * step - 1 + way


def dot(a, b, ca, cb):
    return lax.dot_general(a, b, (((ca,), (cb,)), ((), ())), preferred_element_type=F32)


def kernel(*refs):
    refs = list(refs)

    def take(n):
        out, refs[:n] = refs[:n], []
        return out

    tiles_h, rows_h, cols_h, counts_h, feat, w_in_h, w_out_h, cot_h = take(8)
    logits_h, full_h, small_h = take(3)
    raw = [take(GROUPS), take(GROUPS)]
    picked = take(2)
    sending = take(2)
    tiles, w_in, w_out, cot, rows_s, cols_s, counts_s = take(7)
    far_rows_v, far_rows_s, far_counts_v, far_counts_s = take(4)
    far_tiles, far_spread, far_near, far_acc, far_out, far_in = take(6)
    far_v, far_s, spread, w_in_t, dagg_t, acc1, agg1, acc2, acc3 = take(9)
    agg2_t, logits, red1_out, red1_in, red2_out, red2_in, red3, full = take(8)
    low_out, low_in, low_sum, low_full = take(4)
    sent, y_r, piece_r, b_r, p_r, c_r, last_r, col_s, col_r, row_s, row_r = take(11)
    count_s, count_r, t_r, f_r, ar_r, g4_r, loc = take(7)

    r = lax.axis_index("rep")
    d = lax.axis_index("dom")
    y, k = r // NK, r % NK
    z, x = d // NX, d % NX

    def copy_to(src, dst, s_sem, r_sem, rr, zz, xx):
        copy = pltpu.make_async_remote_copy(
            src_ref=src,
            dst_ref=dst,
            send_sem=s_sem,
            recv_sem=r_sem,
            device_id=(rr, zz * NX + xx),
            device_id_type=pl.DeviceIdType.MESH,
        )
        copy.start()
        return copy

    def wait_bytes(like, sem):
        pltpu.make_async_copy(like, like, sem).wait()

    def send(src, dst, kind, r_sem, rr, zz, xx):
        return copy_to(src, dst, sent.at[kind], r_sem, rr, zz, xx)

    def fetch(i, src, dst):
        copy = pltpu.make_async_copy(src, dst, loc.at[i])
        copy.start()
        return copy

    small = [fetch(0, cols_h, cols_s), fetch(1, rows_h, rows_s), fetch(2, counts_h, counts_s)]
    large = [
        fetch(3, tiles_h, tiles),
        fetch(4, w_in_h, w_in),
        fetch(5, w_out_h, w_out),
        fetch(6, cot_h, cot),
    ]

    greet = [(y * NK + 1 - k, z, x)]
    greet += [(((y + dy) % NY) * NK + k, z, x) for dy in range(1, NY)]
    greet += [(r, z, (x + dx) % NX) for dx in range(1, NX)]
    greet += [(r, (z + dz) % NZ, x) for dz in (1, NZ - 1)]
    barrier = pltpu.get_barrier_semaphore()
    for rr, zz, xx in greet:
        pl.semaphore_signal(
            barrier, inc=1, device_id=(rr, zz * NX + xx), device_id_type=pl.DeviceIdType.MESH
        )
    pl.semaphore_wait(barrier, len(greet))

    half = pl.ds(HALF * k, HALF)
    at = HALF * k + OWN * y

    def ring(p, own, way, step):
        first, count = (0, OWN) if step < STEPS else (way, 1)
        here = pl.ds(at + first, count)
        src = own if step == 1 else raw[p][group_of(way, step - 1)].at[here]
        return send(
            src,
            raw[p][group_of(way, step)].at[here],
            2 + p,
            b_r.at[p, step - 1],
            r,
            (z + (1, NZ - 1)[way]) % NZ,
            x,
        )

    def gather_y(p, own, g):
        here = pl.ds(at, OWN)
        return [
            send(
                own if g == 0 else raw[p][g].at[here],
                raw[p][g].at[here],
                p,
                piece_r.at[p, g, dy - 1] if g in EARLY else y_r.at[p, g],
                ((y + dy) % NY) * NK + k,
                z,
                x,
            )
            for dy in FAR_FIRST
        ]

    def relay(p, way, step, i):
        here = pl.ds(HALF * k + OWN * ((y + NY - i) % NY), OWN)
        g = group_of(way, step)
        return send(
            raw[p][group_of(way, step - 1)].at[here],
            raw[p][g].at[here],
            p,
            y_r.at[p, g],
            r,
            (z + (1, NZ - 1)[way]) % NZ,
            x,
        )

    def share(p, g):
        return send(
            raw[p][g].at[half],
            raw[p][g].at[half],
            4 + p,
            p_r.at[p, g],
            y * NK + 1 - k,
            z,
            x,
        )

    def share_piece(p, g, dy, src=None):
        here = pl.ds(HALF * k + OWN * ((y + NY - dy) % NY), OWN)
        piece = raw[p][g].at[here]
        send(piece if src is None else src, piece, 4 + p, p_r.at[p, g], y * NK + 1 - k, z, x)

    def block(p, g, j):
        return raw[p][g][((j >> 1) & 1) * HALF + (j >> 2) * OWN + (j & 1)]

    def pick(p, g):
        c = ((z + OFFSET[g] + NZ) % NZ) * NX + x
        copies = []
        for dx in FAR_FIRST:
            for s in range(SLOTS):
                sending[p][g, dx - 1, s] = block(p, g, far_s[dx - 1, s, c])
            copies.append(
                send(
                    sending[p].at[g, dx - 1],
                    picked[p].at[g, x],
                    6 + p,
                    last_r.at[dx - 1] if p == 1 and g == LAST else c_r.at[p, g],
                    r,
                    z,
                    (x + dx) % NX,
                )
            )
        for s in range(SLOTS):
            picked[p][g, x, s] = block(p, g, cols_s[s, c])
        return copies

    def exchange(p, own, keep, ready, early, meanwhile, middle, consume):
        rings = {0: [ring(p, own, 0, 1), ring(p, own, 1, 1)]}
        ys = {0: gather_y(p, own, 0)}
        shares, picks = {}, {}
        share_piece(p, 0, 0, own)
        keep()

        def do_z(step):
            wait_bytes(raw[p][0].at[pl.ds(0, 2 * OWN if step < STEPS else OWN)], b_r.at[p, step - 1])
            if step < STEPS:
                rings[step] = [ring(p, own, 0, step + 1), ring(p, own, 1, step + 1)]
            for g in sorted({group_of(0, step), group_of(1, step)}):
                if step != 2 and g != LAST:
                    ys[g] = gather_y(p, own, g)
                if g in EARLY:
                    share_piece(p, g, 0)

        def do_y(g):
            if g in EARLY:
                for dy, copy in zip(FAR_FIRST, ys[g]):
                    copy.wait_recv()
                    share_piece(p, g, dy)
                    if g > 0:
                        relay(p, g - 1, 2, dy)
            else:
                wait_bytes(raw[p][g].at[pl.ds(0, (NY - 1) * OWN)], y_r.at[p, g])
                shares[g] = share(p, g)
            if g == group_of(0, 2):
                for dy in FAR_FIRST:
                    relay(p, 0, 3, dy)

        def do_k(g):
            if g in EARLY:
                wait_bytes(raw[p][g].at[half], p_r.at[p, g])
            else:
                shares[g].wait_recv()
            if g == 0:
                ready()
            picks[g] = pick(p, g)

        def do_c(g):
            wait_bytes(sending[p].at[g], c_r.at[p, g])
            consume(g, range(NX))

        def do_last(g):
            consume(g, [x])
            picks[g][1].wait_recv()
            picks[g][2].wait_recv()
            consume(g, [(x + 1) % NX, (x + NX - 1) % NX])
            picks[g][0].wait_recv()
            consume(g, [(x + 2) % NX])

        def do_w(g):
            if p == 0 and g in MOVED:
                shares[g].wait_recv()
                moved(g)
            else:
                do_k(g)

        meanwhile()
        do_z(1)
        early()
        do_y(0)
        do_w(0)
        do_z(2)
        do_y(1)
        do_w(1)
        do_z(3)
        do_y(2)
        do_w(2)
        middle()
        do_y(3)
        do_z(4)
        do_w(3)
        do_c(0)
        do_y(4)
        do_w(4)
        do_y(6)
        do_w(6)
        do_c(1)
        do_y(7)
        do_w(7)
        do_c(2)
        do_y(LAST)
        do_w(LAST)
        do_c(3)
        do_c(4)
        if p == 1:
            do_c(6)
            do_c(7)
            do_last(LAST)

    tables = []
    for dx in range(1, NX):
        to = (r, z, (x + NX - dx) % NX)
        i = dx - 1
        tables.append(copy_to(cols_h, far_v.at[i], col_s.at[i], col_r.at[i], *to))
        tables.append(copy_to(rows_h, far_rows_v.at[i], row_s.at[i], row_r.at[i], *to))
        tables.append(copy_to(counts_h, far_counts_v.at[i], count_s.at[i], count_r.at[i], *to))

    def block_of(g):
        return ((z + OFFSET[g] + NZ) % NZ) * NX

    def move_tiles():
        for n, g in enumerate(MOVED):
            for dx in (2, 1, 3):
                xx = (x + NX - dx) % NX
                tile = tiles_h.at[block_of(g) + xx]
                send(tile, far_tiles.at[n, dx - 1], 8, t_r.at[0], r, z, xx)

    def early1():
        for copy in tables:
            copy.wait_recv()
        copies = [
            fetch(7, far_v, far_s),
            fetch(9, far_rows_v, far_rows_s),
            fetch(10, far_counts_v, far_counts_s),
        ]
        for copy in copies:
            copy.wait()

    kept = []

    def keep1():
        move_tiles()
        kept.append(fetch(8, feat, raw[0][0].at[pl.ds(at, OWN)]))

    def ready1():
        kept[0].wait()

    def keep2():
        raw[1][0][pl.ds(at, OWN)] = agg1[...]

    def place(into, at, tile, row, live, slot):
        for b in range(OWN):
            into[*at, b * TILE : (b + 1) * TILE, slot * TILE : (slot + 1) * TILE] = jnp.where(
                jnp.logical_and(live, row == b), tile, jnp.zeros_like(tile)
            )

    def meanwhile1():
        for copy in small + large:
            copy.wait()
        for g in range(GROUPS):

            def body(xc, carry, g=g):
                c = block_of(g) + xc
                for t in range(SLOTS):
                    place(spread, (g * NX + xc,), tiles[c, t], rows_s[t, c], t < counts_s[0, c], t)
                return carry

            lax.fori_loop(0, NX, body, 0)
        w_in_t[...] = w_in[...].astype(F32).T.astype(BF)
        dagg_t[...] = dot(w_out[...], cot[...], 1, 1).astype(BF)
        acc1[...] = jnp.zeros_like(acc1)
        acc2[...] = jnp.zeros_like(acc2)
        acc3[...] = jnp.zeros_like(acc3)

    def consume1(g, pieces):
        total = acc1[...]
        for xc in pieces:
            near = picked[0][g, xc].reshape(SLOTS * TILE, TILE)
            total = total + dot(spread[g * NX + xc], near, 1, 0)
        acc1[...] = total

    def middle1():
        wait_bytes(far_tiles, t_r.at[0])
        for n, g in enumerate(MOVED):
            c = block_of(g) + x
            for i in range(NX - 1):
                for t in range(SLOTS):
                    live = t < far_counts_s[i, 0, c]
                    place(far_spread, (n, i), far_tiles[n, i, t], far_rows_s[i, t, c], live, t)

    def moved(g):
        n = MOVED.index(g)
        c = block_of(g) + x
        for i in range(NX - 1):
            for t in range(SLOTS):
                far_near[i, t] = block(0, g, far_s[i, t, c])
            term = dot(far_spread[n, i], far_near[i].reshape(SLOTS * TILE, TILE), 1, 0)
            far_acc[i] = term if n == 0 else far_acc[i] + term
        if n == len(MOVED) - 1:
            far_out[...] = far_acc[...].astype(BF)
            for dx in (2, 1, 3):
                i = dx - 1
                send(far_out.at[i], far_in.at[i], 9, f_r.at[0], r, z, (x + dx) % NX)
        for t in range(SLOTS):
            far_near[NX - 1, t] = block(0, g, cols_s[t, c])
        near = far_near[NX - 1].reshape(SLOTS * TILE, TILE)
        acc1[...] += dot(spread[g * NX + x], near, 1, 0)

    def nothing(g=None):
        pass

    exchange(0, feat, keep1, ready1, early1, meanwhile1, middle1, consume1)
    total = acc1[...]
    wait_bytes(far_in, f_r.at[0])
    for i in range(NX - 1):
        total = total + far_in[i].astype(F32)
    agg1[...] = total.astype(BF).reshape(OWN, TILE, TILE)

    def consume2(g, pieces):
        for xc in pieces:
            near = picked[1][g, xc].reshape(SLOTS * TILE, TILE)
            tile = spread[g * NX + xc]
            z1 = dot(w_in_t[...], near, 1, 1)
            sig = 0.5 + 0.5 * jnp.tanh(0.5 * z1)
            hidden = z1 * sig
            slope = sig + hidden * (1.0 - sig)
            acc2[...] += dot(hidden.astype(BF), tile, 1, 1)
            dz = (dot(dagg_t[...], tile, 1, 0) * slope).astype(BF)
            acc3[...] += dot(dz, near, 1, 0)

    exchange(1, agg1, keep2, nothing, nothing, nothing, nothing, consume2)

    agg2_t[...] = acc2[...].astype(BF)

    def term(core):
        rows = pl.ds(256 * core, 256)
        return (
            dot(agg2_t[rows], cot[...], 1, 0).reshape(SHARE, CHUNK, 512),
            acc3[rows].reshape(SHARE, CHUNK, TILE),
        )

    out, back = term(1 - k)
    red1_out[:, :, 0:512] = out.astype(BF)
    red1_out[:, :, 512:LANES] = back.astype(BF)
    copy = send(red1_out, red1_in, 10, ar_r.at[0], y * NK + 1 - k, z, x)
    out, back = term(k)
    copy.wait_recv()
    red2_out[...] = (out + red1_in[:, :, 0:WIDE].astype(F32)).astype(BF)
    low_out[...] = (back + red1_in[:, :, WIDE:LANES].astype(F32)).astype(BF)

    me = y * NX + x
    plane = [(dy, dx) for dy in range(NY) for dx in range(NX) if dy or dx]
    plane.sort(key=lambda step: -min(step[0], NY - step[0]) - min(step[1], NX - step[1]))
    there = [((y + dy) % NY, (x + dx) % NX) for dy, dx in plane]
    along = [(z + i) % NZ for i in (4, 3, 5, 2, 6, 1, 7)]
    for i, (yy, xx) in enumerate(there):
        send(red2_out.at[yy * NX + xx], red2_in.at[i], 11, ar_r.at[1], yy * NK + k, z, xx)
    for i, zz in enumerate(along):
        send(low_out.at[pl.ds(2 * zz, 2)], low_in.at[i], 12, ar_r.at[2], r, zz, x)
    logits[...] = dot(agg2_t[...], w_out[...], 0, 0).astype(BF)
    done = fetch(0, logits, logits_h)

    wait_bytes(low_in, ar_r.at[2])
    total = low_out[pl.ds(2 * z, 2)].astype(F32)
    for i in range(NZ - 1):
        total = total + low_in[i].astype(F32)
    low_sum[me] = total.astype(BF)
    for yy, xx in there:
        send(low_sum.at[me], low_sum.at[me], 13, ar_r.at[3], yy * NK + k, z, xx)

    wait_bytes(red2_in, ar_r.at[1])
    total = red2_out[me].astype(F32)
    for i in range(PLANE - 1):
        total = total + red2_in[i].astype(F32)
    red3[z] = total.astype(BF)
    for zz in along:
        send(red3.at[z], red3.at[z], 14, ar_r.at[4], r, zz, x)

    wait_bytes(low_sum.at[pl.ds(0, PLANE - 1)], ar_r.at[3])
    total = low_sum[0].astype(F32)
    for i in range(1, PLANE):
        total = total + low_sum[i].astype(F32)
    here = pl.ds(SHARE * k + 2 * z, 2)
    low_full[here] = total.astype(BF)
    for zz in along:
        send(low_full.at[here], low_full.at[here], 15, ar_r.at[5], r, zz, x)

    wait_bytes(red3.at[pl.ds(0, NZ - 1)], ar_r.at[4])
    total = red3[0].astype(F32)
    for i in range(1, NZ):
        total = total + red3[i].astype(F32)
    full[SHARE * k + me] = total.astype(BF)
    chunk = full.at[SHARE * k + me]
    copies = [
        send(chunk, chunk, 16, g4_r.at[i], yy * NK + k, z, xx) for i, (yy, xx) in enumerate(there)
    ]

    def to_core(src, dst, n):
        return send(src, dst, 17 + n, ar_r.at[6 + n], y * NK + 1 - k, z, x)

    to_core(chunk, full_h.at[SHARE * k + me], 0)
    wait_bytes(low_full.at[pl.ds(0, 2 * (NZ - 1))], ar_r.at[5])
    mine = pl.ds(SHARE * k, SHARE)
    to_core(low_full.at[mine], small_h.at[mine], 1)
    last = [fetch(2, low_full.at[mine], small_h.at[mine])]
    for i in range(PLANE - 2, -1, -1):
        copies[i].wait_recv()
        dy, dx = plane[i]
        came = ((y + NY - dy) % NY) * NX + (x + NX - dx) % NX
        to_core(full.at[SHARE * k + came], full_h.at[SHARE * k + came], 0)
    half_full = full.at[mine]
    half_low = low_full.at[mine]
    last.append(fetch(1, half_full, full_h.at[mine]))
    wait_bytes(half_low, ar_r.at[7])
    wait_bytes(half_full, ar_r.at[6])

    for copy in tables:
        copy.wait_send()
    for p in range(2):
        wait_bytes(sending[p], sent.at[p])
        wait_bytes(raw[p][0].at[pl.ds(0, 2 * OWN * (STEPS - 1) + OWN)], sent.at[2 + p])
        wait_bytes(picked[p], sent.at[4 + p])
    wait_bytes(sending[0].at[pl.ds(0, GROUPS - len(MOVED))], sent.at[6])
    wait_bytes(sending[1], sent.at[7])
    wait_bytes(far_tiles, sent.at[8])
    wait_bytes(far_out, sent.at[9])
    wait_bytes(red1_out, sent.at[10])
    wait_bytes(red2_in, sent.at[11])
    wait_bytes(low_in, sent.at[12])
    wait_bytes(low_sum.at[pl.ds(0, PLANE - 1)], sent.at[13])
    wait_bytes(red3.at[pl.ds(0, NZ - 1)], sent.at[14])
    wait_bytes(low_full.at[pl.ds(0, 2 * (NZ - 1))], sent.at[15])
    wait_bytes(red2_in, sent.at[16])
    wait_bytes(half_full, sent.at[17])
    wait_bytes(half_low, sent.at[18])
    done.wait()
    for copy in last:
        copy.wait()


def unpack(logits_in, full, low, logits, grad_in, grad_out):
    logits[...] = logits_in[...]
    grad_out[...] = full[...].astype(F32).reshape(512, WIDE)
    grad_in[...] = low[...].astype(F32).reshape(512, TILE).T


def per_device(
    tile_values, tile_rows, tile_cols, tile_counts, features, weight_in, weight_out, cotangent
):
    vmem = pl.BlockSpec(memory_space=pltpu.VMEM)
    hbm = pl.BlockSpec(memory_space=pltpu.HBM)
    block = pltpu.VMEM((BLOCKS, TILE, TILE), BF)
    dma = pltpu.SemaphoreType.DMA
    scratch = [block] * (2 * GROUPS)
    scratch += [pltpu.VMEM((GROUPS, NX, SLOTS, TILE, TILE), BF)] * 2
    scratch += [pltpu.VMEM((GROUPS, NX - 1, SLOTS, TILE, TILE), BF)] * 2
    scratch += [
        pltpu.VMEM((ND, SLOTS, TILE, TILE), BF),
        pltpu.VMEM((TILE, 512), BF),
        pltpu.VMEM((512, 512), BF),
        pltpu.VMEM((256, 512), BF),
        pltpu.SMEM((SLOTS, ND), jnp.int32),
        pltpu.SMEM((SLOTS, ND), jnp.int32),
        pltpu.SMEM((1, ND), jnp.int32),
        pltpu.VMEM((NX - 1, SLOTS, ND), jnp.int32),
        pltpu.SMEM((NX - 1, SLOTS, ND), jnp.int32),
        pltpu.VMEM((NX - 1, 1, ND), jnp.int32),
        pltpu.SMEM((NX - 1, 1, ND), jnp.int32),
        pltpu.VMEM((len(MOVED), NX - 1, SLOTS, TILE, TILE), BF),
        pltpu.VMEM((len(MOVED), NX - 1, 256, 256), BF),
        pltpu.VMEM((NX, SLOTS, TILE, TILE), BF),
        pltpu.VMEM((NX - 1, 256, TILE), F32),
        pltpu.VMEM((NX - 1, 256, TILE), BF),
        pltpu.VMEM((NX - 1, 256, TILE), BF),
        pltpu.VMEM((NX - 1, SLOTS, ND), jnp.int32),
        pltpu.SMEM((NX - 1, SLOTS, ND), jnp.int32),
        pltpu.VMEM((ND, 256, 256), BF),
        pltpu.VMEM((512, TILE), BF),
        pltpu.VMEM((512, 256), BF),
        pltpu.VMEM((256, TILE), F32),
        pltpu.VMEM((OWN, TILE, TILE), BF),
        pltpu.VMEM((512, 256), F32),
        pltpu.VMEM((512, TILE), F32),
        pltpu.VMEM((512, 256), BF),
        pltpu.VMEM((256, 512), BF),
        pltpu.VMEM((SHARE, CHUNK, LANES), BF),
        pltpu.VMEM((SHARE, CHUNK, LANES), BF),
        pltpu.VMEM((SHARE, CHUNK, WIDE), BF),
        pltpu.VMEM((PLANE - 1, CHUNK, WIDE), BF),
        pltpu.VMEM((NZ, CHUNK, WIDE), BF),
        pltpu.VMEM((CHUNKS, CHUNK, WIDE), BF),
        pltpu.VMEM((SHARE, CHUNK, TILE), BF),
        pltpu.VMEM((NZ - 1, 2, CHUNK, TILE), BF),
        pltpu.VMEM((PLANE, 2, CHUNK, TILE), BF),
        pltpu.VMEM((CHUNKS, CHUNK, TILE), BF),
    ]
    for shape in (
        (19,),
        (2, GROUPS),
        (2, len(EARLY), NY - 1),
        (2, STEPS),
        (2, GROUPS),
        (2, GROUPS),
        (NX - 1,),
    ):
        scratch.append(dma(shape))
    scratch += [dma((NX - 1,))] * 6
    scratch += [dma((1,)), dma((1,)), dma((8,)), dma((PLANE - 1,)), dma((11,))]
    logits, full, low = pl.pallas_call(
        kernel,
        out_shape=(
            jax.ShapeDtypeStruct((256, 512), BF),
            jax.ShapeDtypeStruct((CHUNKS, CHUNK, WIDE), BF),
            jax.ShapeDtypeStruct((CHUNKS, CHUNK, TILE), BF),
        ),
        in_specs=[hbm] * 8,
        out_specs=(hbm,) * 3,
        scratch_shapes=scratch,
        compiler_params=pltpu.CompilerParams(
            collective_id=0, has_side_effects=True, vmem_limit_bytes=60 * 1024 * 1024
        ),
        cost_estimate=pl.CostEstimate(
            flops=5_000_000_000, bytes_accessed=5_000_000, transcendentals=4_000_000
        ),
    )(
        tile_values.reshape(ND, SLOTS, TILE, TILE),
        tile_rows[0, 0].T,
        tile_cols[0, 0].T,
        tile_counts[0],
        features.reshape(OWN, TILE, TILE),
        weight_in,
        weight_out,
        cotangent,
    )
    return pl.pallas_call(
        unpack,
        out_shape=(
            jax.ShapeDtypeStruct((256, 512), BF),
            jax.ShapeDtypeStruct((TILE, 512), F32),
            jax.ShapeDtypeStruct((512, 512), F32),
        ),
        in_specs=[vmem] * 3,
        out_specs=(vmem, vmem, vmem),
        compiler_params=pltpu.CompilerParams(vmem_limit_bytes=60 * 1024 * 1024),
    )(logits, full, low)


def solution(mesh):
    placed = (
        P("rep", "dom", None, None, None, None),
        P("rep", "dom", None, None),
        P("rep", "dom", None, None),
        P("rep", "dom", None),
        P(("dom", "rep"), None),
        P(),
        P(),
        P(("dom", "rep"), None),
    )
    return jax.shard_map(
        per_device,
        mesh=mesh,
        in_specs=placed,
        out_specs=(P(("dom", "rep"), None), P(), P()),
        check_vma=False,
    )
```

```python
import jax
import jax.numpy as jnp
from jax import lax
from jax.experimental import pallas as pl
from jax.experimental.pallas import tpu as pltpu
from jax.sharding import PartitionSpec as P

BF = jnp.bfloat16
F32 = jnp.float32

NY, NK, NZ, NX = 4, 2, 8, 4
NR = NY * NK
ND = NZ * NX
SLOTS = 2
TILE = 128
OWN = 2
BLOCKS = NR * OWN
HALF = BLOCKS // NK
EARLY = (0, 1, 2)
LAST = 5
MOVED = (6, 7, LAST)
STEPS = NZ // 2
GROUPS = NZ
PLANE = NY * NX
FAR_FIRST = (2, 1, 3)
LANES = 640
WIDE = 512
CHUNK = 16
CHUNKS = 512 // CHUNK
SHARE = CHUNKS // NK

OFFSET = [0] + [s * t for t in range(1, STEPS) for s in (-1, 1)] + [STEPS]


def group_of(way, step):
    if step == 0:
        return 0
    if step == STEPS:
        return GROUPS - 1
    return 2 * step - 1 + way


def dot(a, b, ca, cb):
    return lax.dot_general(a, b, (((ca,), (cb,)), ((), ())), preferred_element_type=F32)


def kernel(*refs):
    refs = list(refs)

    def take(n):
        out, refs[:n] = refs[:n], []
        return out

    tiles_h, rows_h, cols_h, counts_h, feat, w_in_h, w_out_h, cot_h = take(8)
    logits_h, full_h, small_h = take(3)
    raw = [take(GROUPS), take(GROUPS)]
    picked = take(2)
    sending = take(2)
    tiles, w_in, w_out, cot, rows_s, cols_s, counts_s = take(7)
    far_rows_v, far_rows_s, far_counts_v, far_counts_s = take(4)
    far_tiles, far_spread, far_near, far_acc, far_out, far_in = take(6)
    far_v, far_s, spread, w_in_t, dagg_t, acc1, agg1, acc2, acc3 = take(9)
    agg2_t, logits, red1_out, red1_in, red2_out, red2_in, red3, full = take(8)
    low_out, low_in, low_sum, low_full = take(4)
    sent, y_r, piece_r, b_r, p_r, c_r, last_r, col_s, col_r, row_s, row_r = take(11)
    count_s, count_r, t_r, f_r, ar_r, g4_r, loc = take(7)

    r = lax.axis_index("rep")
    d = lax.axis_index("dom")
    y, k = r // NK, r % NK
    z, x = d // NX, d % NX

    def copy_to(src, dst, s_sem, r_sem, rr, zz, xx):
        copy = pltpu.make_async_remote_copy(
            src_ref=src,
            dst_ref=dst,
            send_sem=s_sem,
            recv_sem=r_sem,
            device_id=(rr, zz * NX + xx),
            device_id_type=pl.DeviceIdType.MESH,
        )
        copy.start()
        return copy

    def wait_bytes(like, sem):
        pltpu.make_async_copy(like, like, sem).wait()

    def send(src, dst, kind, r_sem, rr, zz, xx):
        return copy_to(src, dst, sent.at[kind], r_sem, rr, zz, xx)

    def fetch(i, src, dst):
        copy = pltpu.make_async_copy(src, dst, loc.at[i])
        copy.start()
        return copy

    small = [fetch(0, cols_h, cols_s), fetch(1, rows_h, rows_s), fetch(2, counts_h, counts_s)]
    large = [
        fetch(3, tiles_h, tiles),
        fetch(4, w_in_h, w_in),
        fetch(5, w_out_h, w_out),
        fetch(6, cot_h, cot),
    ]

    greet = [(y * NK + 1 - k, z, x)]
    greet += [(((y + dy) % NY) * NK + k, z, x) for dy in range(1, NY)]
    greet += [(r, z, (x + dx) % NX) for dx in range(1, NX)]
    greet += [(r, (z + dz) % NZ, x) for dz in (1, NZ - 1)]
    barrier = pltpu.get_barrier_semaphore()
    for rr, zz, xx in greet:
        pl.semaphore_signal(
            barrier, inc=1, device_id=(rr, zz * NX + xx), device_id_type=pl.DeviceIdType.MESH
        )
    pl.semaphore_wait(barrier, len(greet))

    half = pl.ds(HALF * k, HALF)
    at = HALF * k + OWN * y

    def ring(p, own, way, step):
        first, count = (0, OWN) if step < STEPS else (way, 1)
        here = pl.ds(at + first, count)
        src = own if step == 1 else raw[p][group_of(way, step - 1)].at[here]
        return send(
            src,
            raw[p][group_of(way, step)].at[here],
            2 + p,
            b_r.at[p, step - 1],
            r,
            (z + (1, NZ - 1)[way]) % NZ,
            x,
        )

    def gather_y(p, own, g):
        here = pl.ds(at, OWN)
        return [
            send(
                own if g == 0 else raw[p][g].at[here],
                raw[p][g].at[here],
                p,
                piece_r.at[p, g, dy - 1] if g in EARLY else y_r.at[p, g],
                ((y + dy) % NY) * NK + k,
                z,
                x,
            )
            for dy in FAR_FIRST
        ]

    def relay(p, way, step, i):
        here = pl.ds(HALF * k + OWN * ((y + NY - i) % NY), OWN)
        g = group_of(way, step)
        return send(
            raw[p][group_of(way, step - 1)].at[here],
            raw[p][g].at[here],
            p,
            y_r.at[p, g],
            r,
            (z + (1, NZ - 1)[way]) % NZ,
            x,
        )

    def share(p, g):
        return send(
            raw[p][g].at[half],
            raw[p][g].at[half],
            4 + p,
            p_r.at[p, g],
            y * NK + 1 - k,
            z,
            x,
        )

    def share_piece(p, g, dy, src=None):
        here = pl.ds(HALF * k + OWN * ((y + NY - dy) % NY), OWN)
        piece = raw[p][g].at[here]
        send(piece if src is None else src, piece, 4 + p, p_r.at[p, g], y * NK + 1 - k, z, x)

    def block(p, g, j):
        return raw[p][g][((j >> 1) & 1) * HALF + ((j >> 2) & (NY - 1)) * OWN + (j & 1)]

    def pick(p, g):
        c = ((z + OFFSET[g] + NZ) % NZ) * NX + x
        copies = []
        for dx in FAR_FIRST:
            for s in range(SLOTS):
                sending[p][g, dx - 1, s] = block(p, g, far_s[dx - 1, s, c])
            copies.append(
                send(
                    sending[p].at[g, dx - 1],
                    picked[p].at[g, x],
                    6 + p,
                    last_r.at[dx - 1] if p == 1 and g == LAST else c_r.at[p, g],
                    r,
                    z,
                    (x + dx) % NX,
                )
            )
        for s in range(SLOTS):
            picked[p][g, x, s] = block(p, g, cols_s[s, c])
        return copies

    def exchange(p, own, keep, ready, early, meanwhile, middle, consume):
        rings = {0: [ring(p, own, 0, 1), ring(p, own, 1, 1)]}
        ys = {0: gather_y(p, own, 0)}
        shares, picks = {}, {}
        share_piece(p, 0, 0, own)
        keep()

        def do_z(step):
            wait_bytes(raw[p][0].at[pl.ds(0, 2 * OWN if step < STEPS else OWN)], b_r.at[p, step - 1])
            if step < STEPS:
                rings[step] = [ring(p, own, 0, step + 1), ring(p, own, 1, step + 1)]
            for g in sorted({group_of(0, step), group_of(1, step)}):
                if step != 2 and g != LAST:
                    ys[g] = gather_y(p, own, g)
                if g in EARLY:
                    share_piece(p, g, 0)

        def do_y(g):
            if g in EARLY:
                for dy, copy in zip(FAR_FIRST, ys[g]):
                    copy.wait_recv()
                    share_piece(p, g, dy)
                    if g > 0:
                        relay(p, g - 1, 2, dy)
            else:
                wait_bytes(raw[p][g].at[pl.ds(0, (NY - 1) * OWN)], y_r.at[p, g])
                shares[g] = share(p, g)
            if g == group_of(0, 2):
                for dy in FAR_FIRST:
                    relay(p, 0, 3, dy)

        def do_k(g):
            if g in EARLY:
                wait_bytes(raw[p][g].at[half], p_r.at[p, g])
            else:
                shares[g].wait_recv()
            if g == 0:
                ready()
            picks[g] = pick(p, g)

        def do_c(g):
            wait_bytes(sending[p].at[g], c_r.at[p, g])
            consume(g, range(NX))

        def do_last(g):
            consume(g, [x])
            picks[g][1].wait_recv()
            picks[g][2].wait_recv()
            consume(g, [(x + 1) % NX, (x + NX - 1) % NX])
            picks[g][0].wait_recv()
            consume(g, [(x + 2) % NX])

        def do_w(g):
            if p == 0 and g in MOVED:
                shares[g].wait_recv()
                moved(g)
            else:
                do_k(g)

        meanwhile()
        do_z(1)
        early()
        do_y(0)
        do_w(0)
        do_z(2)
        do_y(1)
        do_w(1)
        do_z(3)
        do_y(2)
        do_w(2)
        middle()
        do_y(3)
        do_z(4)
        do_w(3)
        do_c(0)
        do_y(4)
        do_w(4)
        do_y(6)
        do_w(6)
        do_c(1)
        do_y(7)
        do_w(7)
        do_c(2)
        do_y(LAST)
        do_w(LAST)
        do_c(3)
        do_c(4)
        if p == 1:
            do_c(6)
            do_c(7)
            do_last(LAST)

    tables = []
    for dx in range(1, NX):
        to = (r, z, (x + NX - dx) % NX)
        i = dx - 1
        tables.append(copy_to(cols_h, far_v.at[i], col_s.at[i], col_r.at[i], *to))
        tables.append(copy_to(rows_h, far_rows_v.at[i], row_s.at[i], row_r.at[i], *to))
        tables.append(copy_to(counts_h, far_counts_v.at[i], count_s.at[i], count_r.at[i], *to))

    def block_of(g):
        return ((z + OFFSET[g] + NZ) % NZ) * NX

    def move_tiles():
        for n, g in enumerate(MOVED):
            for dx in (2, 1, 3):
                xx = (x + NX - dx) % NX
                tile = tiles_h.at[block_of(g) + xx]
                send(tile, far_tiles.at[n, dx - 1], 8, t_r.at[0], r, z, xx)

    def early1():
        for copy in tables:
            copy.wait_recv()
        copies = [
            fetch(7, far_v, far_s),
            fetch(9, far_rows_v, far_rows_s),
            fetch(10, far_counts_v, far_counts_s),
        ]
        for copy in copies:
            copy.wait()

    kept = []

    def keep1():
        move_tiles()
        kept.append(fetch(8, feat, raw[0][0].at[pl.ds(at, OWN)]))

    def ready1():
        kept[0].wait()

    def keep2():
        raw[1][0][pl.ds(at, OWN)] = agg1[...]

    def place(into, at, tile, row, live, slot):
        for b in range(OWN):
            into[*at, b * TILE : (b + 1) * TILE, slot * TILE : (slot + 1) * TILE] = jnp.where(
                jnp.logical_and(live, row == b), tile, jnp.zeros_like(tile)
            )

    def meanwhile1():
        for copy in small + large:
            copy.wait()
        for g in range(GROUPS):

            def body(xc, carry, g=g):
                c = block_of(g) + xc
                for t in range(SLOTS):
                    place(spread, (g * NX + xc,), tiles[c, t], rows_s[t, c], t < counts_s[0, c], t)
                return carry

            lax.fori_loop(0, NX, body, 0)
        w_in_t[...] = w_in[...].astype(F32).T.astype(BF)
        dagg_t[...] = dot(w_out[...], cot[...], 1, 1).astype(BF)
        acc1[...] = jnp.zeros_like(acc1)
        acc2[...] = jnp.zeros_like(acc2)
        acc3[...] = jnp.zeros_like(acc3)

    def consume1(g, pieces):
        total = acc1[...]
        for xc in pieces:
            near = picked[0][g, xc].reshape(SLOTS * TILE, TILE)
            total = total + dot(spread[g * NX + xc], near, 1, 0)
        acc1[...] = total

    def middle1():
        wait_bytes(far_tiles, t_r.at[0])
        for n, g in enumerate(MOVED):
            c = block_of(g) + x
            for i in range(NX - 1):
                for t in range(SLOTS):
                    live = t < far_counts_s[i, 0, c]
                    place(far_spread, (n, i), far_tiles[n, i, t], far_rows_s[i, t, c], live, t)

    def moved(g):
        n = MOVED.index(g)
        c = block_of(g) + x
        for dx in FAR_FIRST:
            i = dx - 1
            for t in range(SLOTS):
                far_near[i, t] = block(0, g, far_s[i, t, c])
            term = dot(far_spread[n, i], far_near[i].reshape(SLOTS * TILE, TILE), 1, 0)
            term = term if n == 0 else far_acc[i] + term
            if n < len(MOVED) - 1:
                far_acc[i] = term
            else:
                far_out[i] = term.astype(BF)
                send(far_out.at[i], far_in.at[i], 9, f_r.at[0], r, z, (x + dx) % NX)
        for t in range(SLOTS):
            far_near[NX - 1, t] = block(0, g, cols_s[t, c])
        near = far_near[NX - 1].reshape(SLOTS * TILE, TILE)
        acc1[...] += dot(spread[g * NX + x], near, 1, 0)

    def nothing(g=None):
        pass

    exchange(0, feat, keep1, ready1, early1, meanwhile1, middle1, consume1)
    total = acc1[...]
    wait_bytes(far_in, f_r.at[0])
    for i in range(NX - 1):
        total = total + far_in[i].astype(F32)
    agg1[...] = total.astype(BF).reshape(OWN, TILE, TILE)

    def consume2(g, pieces):
        for xc in pieces:
            near = picked[1][g, xc].reshape(SLOTS * TILE, TILE)
            tile = spread[g * NX + xc]
            z1 = dot(w_in_t[...], near, 1, 1)
            sig = 0.5 + 0.5 * jnp.tanh(0.5 * z1)
            hidden = z1 * sig
            slope = sig + hidden * (1.0 - sig)
            acc2[...] += dot(hidden.astype(BF), tile, 1, 1)
            dz = (dot(dagg_t[...], tile, 1, 0) * slope).astype(BF)
            acc3[...] += dot(dz, near, 1, 0)

    exchange(1, agg1, keep2, nothing, nothing, nothing, nothing, consume2)

    agg2_t[...] = acc2[...].astype(BF)

    def term(core):
        rows = pl.ds(256 * core, 256)
        return (
            dot(agg2_t[rows], cot[...], 1, 0).reshape(SHARE, CHUNK, 512),
            acc3[rows].reshape(SHARE, CHUNK, TILE),
        )

    out, back = term(1 - k)
    red1_out[:, :, 0:512] = out.astype(BF)
    red1_out[:, :, 512:LANES] = back.astype(BF)
    copy = send(red1_out, red1_in, 10, ar_r.at[0], y * NK + 1 - k, z, x)
    out, back = term(k)
    copy.wait_recv()
    red2_out[...] = (out + red1_in[:, :, 0:WIDE].astype(F32)).astype(BF)
    low_out[...] = (back + red1_in[:, :, WIDE:LANES].astype(F32)).astype(BF)

    me = y * NX + x
    plane = [(dy, dx) for dy in range(NY) for dx in range(NX) if dy or dx]
    plane.sort(key=lambda step: -min(step[0], NY - step[0]) - min(step[1], NX - step[1]))
    there = [((y + dy) % NY, (x + dx) % NX) for dy, dx in plane]
    along = [(z + i) % NZ for i in (4, 3, 5, 2, 6, 1, 7)]
    for i, (yy, xx) in enumerate(there):
        send(red2_out.at[yy * NX + xx], red2_in.at[i], 11, ar_r.at[1], yy * NK + k, z, xx)
    for i, zz in enumerate(along):
        send(low_out.at[pl.ds(2 * zz, 2)], low_in.at[i], 12, ar_r.at[2], r, zz, x)
    logits[...] = dot(agg2_t[...], w_out[...], 0, 0).astype(BF)
    done = fetch(0, logits, logits_h)

    wait_bytes(low_in, ar_r.at[2])
    total = low_out[pl.ds(2 * z, 2)].astype(F32)
    for i in range(NZ - 1):
        total = total + low_in[i].astype(F32)
    low_sum[me] = total.astype(BF)
    for yy, xx in there:
        send(low_sum.at[me], low_sum.at[me], 13, ar_r.at[3], yy * NK + k, z, xx)

    wait_bytes(red2_in, ar_r.at[1])
    total = red2_out[me].astype(F32)
    for i in range(PLANE - 1):
        total = total + red2_in[i].astype(F32)
    red3[z] = total.astype(BF)
    for zz in along:
        send(red3.at[z], red3.at[z], 14, ar_r.at[4], r, zz, x)

    wait_bytes(low_sum.at[pl.ds(0, PLANE - 1)], ar_r.at[3])
    total = low_sum[0].astype(F32)
    for i in range(1, PLANE):
        total = total + low_sum[i].astype(F32)
    here = pl.ds(SHARE * k + 2 * z, 2)
    low_full[here] = total.astype(BF)
    for zz in along:
        send(low_full.at[here], low_full.at[here], 15, ar_r.at[5], r, zz, x)

    wait_bytes(red3.at[pl.ds(0, NZ - 1)], ar_r.at[4])
    total = red3[0].astype(F32)
    for i in range(1, NZ):
        total = total + red3[i].astype(F32)
    full[SHARE * k + me] = total.astype(BF)
    chunk = full.at[SHARE * k + me]
    copies = [
        send(chunk, chunk, 16, g4_r.at[i], yy * NK + k, z, xx) for i, (yy, xx) in enumerate(there)
    ]

    def to_core(src, dst, n):
        return send(src, dst, 17 + n, ar_r.at[6 + n], y * NK + 1 - k, z, x)

    to_core(chunk, full_h.at[SHARE * k + me], 0)
    wait_bytes(low_full.at[pl.ds(0, 2 * (NZ - 1))], ar_r.at[5])
    mine = pl.ds(SHARE * k, SHARE)
    to_core(low_full.at[mine], small_h.at[mine], 1)
    last = [fetch(2, low_full.at[mine], small_h.at[mine])]
    for i in range(PLANE - 2, -1, -1):
        copies[i].wait_recv()
        dy, dx = plane[i]
        came = ((y + NY - dy) % NY) * NX + (x + NX - dx) % NX
        to_core(full.at[SHARE * k + came], full_h.at[SHARE * k + came], 0)
    half_full = full.at[mine]
    half_low = low_full.at[mine]
    last.append(fetch(1, half_full, full_h.at[mine]))
    wait_bytes(half_low, ar_r.at[7])
    wait_bytes(half_full, ar_r.at[6])

    for copy in tables:
        copy.wait_send()
    for p in range(2):
        wait_bytes(sending[p], sent.at[p])
        wait_bytes(raw[p][0].at[pl.ds(0, 2 * OWN * (STEPS - 1) + OWN)], sent.at[2 + p])
        wait_bytes(picked[p], sent.at[4 + p])
    wait_bytes(sending[0].at[pl.ds(0, GROUPS - len(MOVED))], sent.at[6])
    wait_bytes(sending[1], sent.at[7])
    wait_bytes(far_tiles, sent.at[8])
    wait_bytes(far_out, sent.at[9])
    wait_bytes(red1_out, sent.at[10])
    wait_bytes(red2_in, sent.at[11])
    wait_bytes(low_in, sent.at[12])
    wait_bytes(low_sum.at[pl.ds(0, PLANE - 1)], sent.at[13])
    wait_bytes(red3.at[pl.ds(0, NZ - 1)], sent.at[14])
    wait_bytes(low_full.at[pl.ds(0, 2 * (NZ - 1))], sent.at[15])
    wait_bytes(red2_in, sent.at[16])
    wait_bytes(half_full, sent.at[17])
    wait_bytes(half_low, sent.at[18])
    done.wait()
    for copy in last:
        copy.wait()


def unpack(logits_in, full, low, logits, grad_in, grad_out):
    logits[...] = logits_in[...]
    grad_out[...] = full[...].astype(F32).reshape(512, WIDE)
    grad_in[...] = low[...].astype(F32).reshape(512, TILE).T


def per_device(
    tile_values, tile_rows, tile_cols, tile_counts, features, weight_in, weight_out, cotangent
):
    vmem = pl.BlockSpec(memory_space=pltpu.VMEM)
    hbm = pl.BlockSpec(memory_space=pltpu.HBM)
    block = pltpu.VMEM((BLOCKS, TILE, TILE), BF)
    dma = pltpu.SemaphoreType.DMA
    scratch = [block] * (2 * GROUPS)
    scratch += [pltpu.VMEM((GROUPS, NX, SLOTS, TILE, TILE), BF)] * 2
    scratch += [pltpu.VMEM((GROUPS, NX - 1, SLOTS, TILE, TILE), BF)] * 2
    scratch += [
        pltpu.VMEM((ND, SLOTS, TILE, TILE), BF),
        pltpu.VMEM((TILE, 512), BF),
        pltpu.VMEM((512, 512), BF),
        pltpu.VMEM((256, 512), BF),
        pltpu.SMEM((SLOTS, ND), jnp.int32),
        pltpu.SMEM((SLOTS, ND), jnp.int32),
        pltpu.SMEM((1, ND), jnp.int32),
        pltpu.VMEM((NX - 1, SLOTS, ND), jnp.int32),
        pltpu.SMEM((NX - 1, SLOTS, ND), jnp.int32),
        pltpu.VMEM((NX - 1, 1, ND), jnp.int32),
        pltpu.SMEM((NX - 1, 1, ND), jnp.int32),
        pltpu.VMEM((len(MOVED), NX - 1, SLOTS, TILE, TILE), BF),
        pltpu.VMEM((len(MOVED), NX - 1, 256, 256), BF),
        pltpu.VMEM((NX, SLOTS, TILE, TILE), BF),
        pltpu.VMEM((NX - 1, 256, TILE), F32),
        pltpu.VMEM((NX - 1, 256, TILE), BF),
        pltpu.VMEM((NX - 1, 256, TILE), BF),
        pltpu.VMEM((NX - 1, SLOTS, ND), jnp.int32),
        pltpu.SMEM((NX - 1, SLOTS, ND), jnp.int32),
        pltpu.VMEM((ND, 256, 256), BF),
        pltpu.VMEM((512, TILE), BF),
        pltpu.VMEM((512, 256), BF),
        pltpu.VMEM((256, TILE), F32),
        pltpu.VMEM((OWN, TILE, TILE), BF),
        pltpu.VMEM((512, 256), F32),
        pltpu.VMEM((512, TILE), F32),
        pltpu.VMEM((512, 256), BF),
        pltpu.VMEM((256, 512), BF),
        pltpu.VMEM((SHARE, CHUNK, LANES), BF),
        pltpu.VMEM((SHARE, CHUNK, LANES), BF),
        pltpu.VMEM((SHARE, CHUNK, WIDE), BF),
        pltpu.VMEM((PLANE - 1, CHUNK, WIDE), BF),
        pltpu.VMEM((NZ, CHUNK, WIDE), BF),
        pltpu.VMEM((CHUNKS, CHUNK, WIDE), BF),
        pltpu.VMEM((SHARE, CHUNK, TILE), BF),
        pltpu.VMEM((NZ - 1, 2, CHUNK, TILE), BF),
        pltpu.VMEM((PLANE, 2, CHUNK, TILE), BF),
        pltpu.VMEM((CHUNKS, CHUNK, TILE), BF),
    ]
    for shape in (
        (19,),
        (2, GROUPS),
        (2, len(EARLY), NY - 1),
        (2, STEPS),
        (2, GROUPS),
        (2, GROUPS),
        (NX - 1,),
    ):
        scratch.append(dma(shape))
    scratch += [dma((NX - 1,))] * 6
    scratch += [dma((1,)), dma((1,)), dma((8,)), dma((PLANE - 1,)), dma((11,))]
    logits, full, low = pl.pallas_call(
        kernel,
        out_shape=(
            jax.ShapeDtypeStruct((256, 512), BF),
            jax.ShapeDtypeStruct((CHUNKS, CHUNK, WIDE), BF),
            jax.ShapeDtypeStruct((CHUNKS, CHUNK, TILE), BF),
        ),
        in_specs=[hbm] * 8,
        out_specs=(hbm,) * 3,
        scratch_shapes=scratch,
        compiler_params=pltpu.CompilerParams(
            collective_id=0, has_side_effects=True, vmem_limit_bytes=60 * 1024 * 1024
        ),
        cost_estimate=pl.CostEstimate(
            flops=5_000_000_000, bytes_accessed=5_000_000, transcendentals=4_000_000
        ),
    )(
        tile_values.reshape(ND, SLOTS, TILE, TILE),
        tile_rows[0, 0].T,
        tile_cols[0, 0].T,
        tile_counts[0],
        features.reshape(OWN, TILE, TILE),
        weight_in,
        weight_out,
        cotangent,
    )
    return pl.pallas_call(
        unpack,
        out_shape=(
            jax.ShapeDtypeStruct((256, 512), BF),
            jax.ShapeDtypeStruct((TILE, 512), F32),
            jax.ShapeDtypeStruct((512, 512), F32),
        ),
        in_specs=[vmem] * 3,
        out_specs=(vmem, vmem, vmem),
        compiler_params=pltpu.CompilerParams(vmem_limit_bytes=60 * 1024 * 1024),
    )(logits, full, low)


def solution(mesh):
    placed = (
        P("rep", "dom", None, None, None, None),
        P("rep", "dom", None, None),
        P("rep", "dom", None, None),
        P("rep", "dom", None),
        P(("dom", "rep"), None),
        P(),
        P(),
        P(("dom", "rep"), None),
    )
    return jax.shard_map(
        per_device,
        mesh=mesh,
        in_specs=placed,
        out_specs=(P(("dom", "rep"), None), P(), P()),
        check_vma=False,
    )
```

```python
import jax
import jax.numpy as jnp
from jax import lax
from jax.experimental import pallas as pl
from jax.experimental.pallas import tpu as pltpu
from jax.sharding import PartitionSpec as P

BF = jnp.bfloat16
F32 = jnp.float32

NY, NK, NZ, NX = 4, 2, 8, 4
NR = NY * NK
ND = NZ * NX
SLOTS = 2
TILE = 128
OWN = 2
BLOCKS = NR * OWN
HALF = BLOCKS // NK
EARLY = (0, 1, 2)
LAST = 5
MOVED = (6, 7, LAST)
STEPS = NZ // 2
GROUPS = NZ
PLANE = NY * NX
FAR_FIRST = (2, 1, 3)
LANES = 640
WIDE = 512
CHUNK = 16
CHUNKS = 512 // CHUNK
SHARE = CHUNKS // NK

OFFSET = [0] + [s * t for t in range(1, STEPS) for s in (-1, 1)] + [STEPS]


def group_of(way, step):
    if step == 0:
        return 0
    if step == STEPS:
        return GROUPS - 1
    return 2 * step - 1 + way


def dot(a, b, ca, cb):
    return lax.dot_general(a, b, (((ca,), (cb,)), ((), ())), preferred_element_type=F32)


def kernel(*refs):
    refs = list(refs)

    def take(n):
        out, refs[:n] = refs[:n], []
        return out

    tiles_h, rows_h, cols_h, counts_h, feat, w_in_h, w_out_h, cot_h = take(8)
    logits_h, full_h, small_h = take(3)
    raw = [take(GROUPS), take(GROUPS)]
    picked = take(2)
    sending = take(2)
    tiles, w_in, w_out, cot, rows_s, cols_s, counts_s = take(7)
    far_rows_v, far_rows_s, far_counts_v, far_counts_s = take(4)
    far_tiles, far_spread, far_near, far_acc, far_out, far_in = take(6)
    far_v, far_s, spread, w_in_t, dagg_t, acc1, agg1, acc2, acc3 = take(9)
    agg2_t, logits, red1_out, red1_in, red2_out, red2_in, red3, full = take(8)
    low_out, low_in, low_sum, low_full = take(4)
    sent, y_r, piece_r, b_r, p_r, c_r, last_r, col_s, col_r, row_s, row_r = take(11)
    count_s, count_r, t_r, f_r, ar_r, g4_r, loc = take(7)

    r = lax.axis_index("rep")
    d = lax.axis_index("dom")
    y, k = r // NK, r % NK
    z, x = d // NX, d % NX

    def copy_to(src, dst, s_sem, r_sem, rr, zz, xx):
        copy = pltpu.make_async_remote_copy(
            src_ref=src,
            dst_ref=dst,
            send_sem=s_sem,
            recv_sem=r_sem,
            device_id=(rr, zz * NX + xx),
            device_id_type=pl.DeviceIdType.MESH,
        )
        copy.start()
        return copy

    def wait_bytes(like, sem):
        pltpu.make_async_copy(like, like, sem).wait()

    def send(src, dst, kind, r_sem, rr, zz, xx):
        return copy_to(src, dst, sent.at[kind], r_sem, rr, zz, xx)

    def fetch(i, src, dst):
        copy = pltpu.make_async_copy(src, dst, loc.at[i])
        copy.start()
        return copy

    small = [fetch(0, cols_h, cols_s), fetch(1, rows_h, rows_s), fetch(2, counts_h, counts_s)]
    large = [
        fetch(3, tiles_h, tiles),
        fetch(4, w_in_h, w_in),
        fetch(5, w_out_h, w_out),
        fetch(6, cot_h, cot),
    ]

    greet = [(y * NK + 1 - k, z, x)]
    greet += [(((y + dy) % NY) * NK + k, z, x) for dy in range(1, NY)]
    greet += [(r, z, (x + dx) % NX) for dx in range(1, NX)]
    greet += [(r, (z + dz) % NZ, x) for dz in (1, NZ - 1)]
    barrier = pltpu.get_barrier_semaphore()
    for rr, zz, xx in greet:
        pl.semaphore_signal(
            barrier, inc=1, device_id=(rr, zz * NX + xx), device_id_type=pl.DeviceIdType.MESH
        )
    pl.semaphore_wait(barrier, len(greet))

    half = pl.ds(HALF * k, HALF)
    at = HALF * k + OWN * y

    def ring(p, own, way, step):
        first, count = (0, OWN) if step < STEPS else (way, 1)
        here = pl.ds(at + first, count)
        src = own if step == 1 else raw[p][group_of(way, step - 1)].at[here]
        return send(
            src,
            raw[p][group_of(way, step)].at[here],
            2 + p,
            b_r.at[p, step - 1],
            r,
            (z + (1, NZ - 1)[way]) % NZ,
            x,
        )

    def gather_y(p, own, g):
        here = pl.ds(at, OWN)
        return [
            send(
                own if g == 0 else raw[p][g].at[here],
                raw[p][g].at[here],
                p,
                piece_r.at[p, g, dy - 1] if g in EARLY else y_r.at[p, g],
                ((y + dy) % NY) * NK + k,
                z,
                x,
            )
            for dy in FAR_FIRST
        ]

    def relay(p, way, step, i):
        here = pl.ds(HALF * k + OWN * ((y + NY - i) % NY), OWN)
        g = group_of(way, step)
        return send(
            raw[p][group_of(way, step - 1)].at[here],
            raw[p][g].at[here],
            p,
            y_r.at[p, g],
            r,
            (z + (1, NZ - 1)[way]) % NZ,
            x,
        )

    def share(p, g):
        return send(
            raw[p][g].at[half],
            raw[p][g].at[half],
            4 + p,
            p_r.at[p, g],
            y * NK + 1 - k,
            z,
            x,
        )

    def share_piece(p, g, dy, src=None):
        here = pl.ds(HALF * k + OWN * ((y + NY - dy) % NY), OWN)
        piece = raw[p][g].at[here]
        send(piece if src is None else src, piece, 4 + p, p_r.at[p, g], y * NK + 1 - k, z, x)

    def block(p, g, j):
        return raw[p][g][((j >> 1) & 1) * HALF + ((j >> 2) & (NY - 1)) * OWN + (j & 1)]

    def pick(p, g):
        c = ((z + OFFSET[g] + NZ) % NZ) * NX + x
        copies = []
        for dx in FAR_FIRST:
            for s in range(SLOTS):
                sending[p][g, dx - 1, s] = block(p, g, far_s[dx - 1, s, c])
            copies.append(
                send(
                    sending[p].at[g, dx - 1],
                    picked[p].at[g, x],
                    6 + p,
                    last_r.at[dx - 1] if p == 1 and g == LAST else c_r.at[p, g],
                    r,
                    z,
                    (x + dx) % NX,
                )
            )
        for s in range(SLOTS):
            picked[p][g, x, s] = block(p, g, cols_s[s, c])
        return copies

    def exchange(p, own, keep, ready, early, meanwhile, middle, consume):
        rings = {0: [ring(p, own, 0, 1), ring(p, own, 1, 1)]}
        ys = {0: gather_y(p, own, 0)}
        shares, picks = {}, {}
        share_piece(p, 0, 0, own)
        keep()

        def do_z(step):
            wait_bytes(raw[p][0].at[pl.ds(0, 2 * OWN if step < STEPS else OWN)], b_r.at[p, step - 1])
            if step < STEPS:
                rings[step] = [ring(p, own, 0, step + 1), ring(p, own, 1, step + 1)]
            for g in sorted({group_of(0, step), group_of(1, step)}):
                if step != 2 and g != LAST:
                    ys[g] = gather_y(p, own, g)
                if g in EARLY:
                    share_piece(p, g, 0)

        def do_y(g):
            if g in EARLY:
                for dy, copy in zip(FAR_FIRST, ys[g]):
                    copy.wait_recv()
                    share_piece(p, g, dy)
                    if g > 0:
                        relay(p, g - 1, 2, dy)
            else:
                wait_bytes(raw[p][g].at[pl.ds(0, (NY - 1) * OWN)], y_r.at[p, g])
                shares[g] = share(p, g)
            if g == group_of(0, 2):
                for dy in FAR_FIRST:
                    relay(p, 0, 3, dy)

        def do_k(g):
            if g in EARLY:
                wait_bytes(raw[p][g].at[half], p_r.at[p, g])
            else:
                shares[g].wait_recv()
            if g == 0:
                ready()
            picks[g] = pick(p, g)

        def do_c(g):
            wait_bytes(sending[p].at[g], c_r.at[p, g])
            consume(g, range(NX))

        def do_last(g):
            consume(g, [x])
            picks[g][1].wait_recv()
            picks[g][2].wait_recv()
            consume(g, [(x + 1) % NX, (x + NX - 1) % NX])
            picks[g][0].wait_recv()
            consume(g, [(x + 2) % NX])

        def do_w(g):
            if p == 0 and g in MOVED:
                shares[g].wait_recv()
                moved(g)
            else:
                do_k(g)

        meanwhile()
        do_z(1)
        early()
        do_y(0)
        do_w(0)
        do_z(2)
        do_y(1)
        do_w(1)
        do_z(3)
        do_y(2)
        do_w(2)
        middle()
        do_y(3)
        do_z(4)
        do_w(3)
        do_c(0)
        do_y(4)
        do_w(4)
        do_y(6)
        do_w(6)
        do_c(1)
        do_y(7)
        do_w(7)
        do_c(2)
        do_y(LAST)
        do_w(LAST)
        do_c(3)
        do_c(4)
        if p == 1:
            do_c(6)
            do_c(7)
            do_last(LAST)

    tables = []
    for dx in range(1, NX):
        to = (r, z, (x + NX - dx) % NX)
        i = dx - 1
        tables.append(copy_to(cols_h, far_v.at[i], col_s.at[i], col_r.at[i], *to))
        tables.append(copy_to(rows_h, far_rows_v.at[i], row_s.at[i], row_r.at[i], *to))
        tables.append(copy_to(counts_h, far_counts_v.at[i], count_s.at[i], count_r.at[i], *to))

    def block_of(g):
        return ((z + OFFSET[g] + NZ) % NZ) * NX

    def move_tiles():
        for n, g in enumerate(MOVED):
            for dx in (2, 1, 3):
                xx = (x + NX - dx) % NX
                tile = tiles_h.at[block_of(g) + xx]
                send(tile, far_tiles.at[n, dx - 1], 8, t_r.at[0], r, z, xx)

    def early1():
        for copy in tables:
            copy.wait_recv()
        copies = [
            fetch(7, far_v, far_s),
            fetch(9, far_rows_v, far_rows_s),
            fetch(10, far_counts_v, far_counts_s),
        ]
        for copy in copies:
            copy.wait()

    kept = []

    def keep1():
        move_tiles()
        kept.append(fetch(8, feat, raw[0][0].at[pl.ds(at, OWN)]))

    def ready1():
        kept[0].wait()

    def keep2():
        raw[1][0][pl.ds(at, OWN)] = agg1[...]

    def place(into, at, tile, row, live, slot):
        for b in range(OWN):
            into[*at, b * TILE : (b + 1) * TILE, slot * TILE : (slot + 1) * TILE] = jnp.where(
                jnp.logical_and(live, row == b), tile, jnp.zeros_like(tile)
            )

    def meanwhile1():
        for copy in small + large:
            copy.wait()
        for g in range(GROUPS):

            def body(xc, carry, g=g):
                c = block_of(g) + xc
                for t in range(SLOTS):
                    place(spread, (g * NX + xc,), tiles[c, t], rows_s[t, c], t < counts_s[0, c], t)
                return carry

            lax.fori_loop(0, NX, body, 0)
        w_in_t[...] = w_in[...].astype(F32).T.astype(BF)
        dagg_t[...] = dot(w_out[...], cot[...], 1, 1).astype(BF)
        acc1[...] = jnp.zeros_like(acc1)
        acc2[...] = jnp.zeros_like(acc2)
        acc3[...] = jnp.zeros_like(acc3)

    def consume1(g, pieces):
        total = acc1[...]
        for xc in pieces:
            near = picked[0][g, xc].reshape(SLOTS * TILE, TILE)
            total = total + dot(spread[g * NX + xc], near, 1, 0)
        acc1[...] = total

    def middle1():
        wait_bytes(far_tiles, t_r.at[0])
        for n, g in enumerate(MOVED):
            c = block_of(g) + x
            for i in range(NX - 1):
                for t in range(SLOTS):
                    live = t < far_counts_s[i, 0, c]
                    place(far_spread, (n, i), far_tiles[n, i, t], far_rows_s[i, t, c], live, t)

    def moved(g):
        n = MOVED.index(g)
        c = block_of(g) + x
        for dx in FAR_FIRST:
            i = dx - 1
            for t in range(SLOTS):
                far_near[i, t] = block(0, g, far_s[i, t, c])
            term = dot(far_spread[n, i], far_near[i].reshape(SLOTS * TILE, TILE), 1, 0)
            term = term if n == 0 else far_acc[i] + term
            if n < len(MOVED) - 1:
                far_acc[i] = term
            else:
                far_out[i] = term.astype(BF)
                send(far_out.at[i], far_in.at[i], 9, f_r.at[0], r, z, (x + dx) % NX)
        for t in range(SLOTS):
            far_near[NX - 1, t] = block(0, g, cols_s[t, c])
        near = far_near[NX - 1].reshape(SLOTS * TILE, TILE)
        acc1[...] += dot(spread[g * NX + x], near, 1, 0)

    def nothing(g=None):
        pass

    exchange(0, feat, keep1, ready1, early1, meanwhile1, middle1, consume1)
    total = acc1[...]
    wait_bytes(far_in, f_r.at[0])
    for i in range(NX - 1):
        total = total + far_in[i].astype(F32)
    agg1[...] = total.astype(BF).reshape(OWN, TILE, TILE)

    def consume2(g, pieces):
        for xc in pieces:
            near = picked[1][g, xc].reshape(SLOTS * TILE, TILE)
            tile = spread[g * NX + xc]
            z1 = dot(w_in_t[...], near, 1, 1)
            sig = 0.5 + 0.5 * jnp.tanh(0.5 * z1)
            hidden = z1 * sig
            slope = sig + hidden * (1.0 - sig)
            acc2[...] += dot(hidden.astype(BF), tile, 1, 1)
            dz = (dot(dagg_t[...], tile, 1, 0) * slope).astype(BF)
            acc3[...] += dot(dz, near, 1, 0)

    exchange(1, agg1, keep2, nothing, nothing, nothing, nothing, consume2)

    agg2_t[...] = acc2[...].astype(BF)

    def term(core):
        rows = pl.ds(256 * core, 256)
        return (
            dot(agg2_t[rows], cot[...], 1, 0).reshape(SHARE, CHUNK, 512),
            acc3[rows].reshape(SHARE, CHUNK, TILE),
        )

    out, back = term(1 - k)
    red1_out[:, :, 0:512] = out.astype(BF)
    red1_out[:, :, 512:LANES] = back.astype(BF)
    copy = send(red1_out, red1_in, 10, ar_r.at[0], y * NK + 1 - k, z, x)
    out, back = term(k)
    copy.wait_recv()
    red2_out[...] = (out + red1_in[:, :, 0:WIDE].astype(F32)).astype(BF)
    low_out[...] = (back + red1_in[:, :, WIDE:LANES].astype(F32)).astype(BF)

    me = y * NX + x
    plane = [(dy, dx) for dy in range(NY) for dx in range(NX) if dy or dx]
    plane.sort(key=lambda step: -min(step[0], NY - step[0]) - min(step[1], NX - step[1]))
    there = [((y + dy) % NY, (x + dx) % NX) for dy, dx in plane]
    along = [(z + i) % NZ for i in (4, 3, 5, 2, 6, 1, 7)]
    for i, (yy, xx) in enumerate(there):
        send(red2_out.at[yy * NX + xx], red2_in.at[i], 11, ar_r.at[1], yy * NK + k, z, xx)
    for i, zz in enumerate(along):
        send(low_out.at[pl.ds(2 * zz, 2)], low_in.at[i], 12, ar_r.at[2], r, zz, x)
    logits[...] = dot(agg2_t[...], w_out[...], 0, 0).astype(BF)
    done = fetch(0, logits, logits_h)

    wait_bytes(low_in, ar_r.at[2])
    total = low_out[pl.ds(2 * z, 2)].astype(F32)
    for i in range(NZ - 1):
        total = total + low_in[i].astype(F32)
    low_sum[me] = total.astype(BF)
    for yy, xx in there:
        send(low_sum.at[me], low_sum.at[me], 13, ar_r.at[3], yy * NK + k, z, xx)

    wait_bytes(red2_in, ar_r.at[1])
    total = red2_out[me].astype(F32)
    for i in range(PLANE - 1):
        total = total + red2_in[i].astype(F32)
    red3[z] = total.astype(BF)
    for zz in along:
        send(red3.at[z], red3.at[z], 14, ar_r.at[4], r, zz, x)

    wait_bytes(low_sum.at[pl.ds(0, PLANE - 1)], ar_r.at[3])
    total = low_sum[0].astype(F32)
    for i in range(1, PLANE):
        total = total + low_sum[i].astype(F32)
    here = pl.ds(SHARE * k + 2 * z, 2)
    low_full[here] = total.astype(BF)
    for zz in along:
        send(low_full.at[here], low_full.at[here], 15, ar_r.at[5], r, zz, x)

    wait_bytes(red3.at[pl.ds(0, NZ - 1)], ar_r.at[4])
    total = red3[0].astype(F32)
    for i in range(1, NZ):
        total = total + red3[i].astype(F32)
    full[SHARE * k + me] = total.astype(BF)
    chunk = full.at[SHARE * k + me]
    copies = [
        send(chunk, chunk, 16, g4_r.at[i], yy * NK + k, z, xx) for i, (yy, xx) in enumerate(there)
    ]

    def to_core(src, dst, n):
        return send(src, dst, 17 + n, ar_r.at[6 + n], y * NK + 1 - k, z, x)

    to_core(chunk, full_h.at[SHARE * k + me], 0)
    wait_bytes(low_full.at[pl.ds(0, 2 * (NZ - 1))], ar_r.at[5])
    mine = pl.ds(SHARE * k, SHARE)
    to_core(low_full.at[mine], small_h.at[mine], 1)
    last = [fetch(2, low_full.at[mine], small_h.at[mine])]
    for i in range(PLANE - 2, -1, -1):
        copies[i].wait_recv()
        dy, dx = plane[i]
        came = ((y + NY - dy) % NY) * NX + (x + NX - dx) % NX
        to_core(full.at[SHARE * k + came], full_h.at[SHARE * k + came], 0)
    half_full = full.at[mine]
    half_low = low_full.at[mine]
    last.append(fetch(1, half_full, full_h.at[mine]))
    wait_bytes(half_low, ar_r.at[7])
    wait_bytes(half_full, ar_r.at[6])

    for copy in tables:
        copy.wait_send()
    for p in range(2):
        wait_bytes(sending[p], sent.at[p])
        wait_bytes(raw[p][0].at[pl.ds(0, 2 * OWN * (STEPS - 1) + OWN)], sent.at[2 + p])
        wait_bytes(picked[p], sent.at[4 + p])
    wait_bytes(sending[0].at[pl.ds(0, GROUPS - len(MOVED))], sent.at[6])
    wait_bytes(sending[1], sent.at[7])
    wait_bytes(far_tiles, sent.at[8])
    wait_bytes(far_out, sent.at[9])
    wait_bytes(red1_out, sent.at[10])
    wait_bytes(red2_in, sent.at[11])
    wait_bytes(low_in, sent.at[12])
    wait_bytes(low_sum.at[pl.ds(0, PLANE - 1)], sent.at[13])
    wait_bytes(red3.at[pl.ds(0, NZ - 1)], sent.at[14])
    wait_bytes(low_full.at[pl.ds(0, 2 * (NZ - 1))], sent.at[15])
    wait_bytes(red2_in, sent.at[16])
    wait_bytes(half_full, sent.at[17])
    wait_bytes(half_low, sent.at[18])
    done.wait()
    for copy in last:
        copy.wait()


def unpack(logits_in, full, low, logits, grad_in, grad_out):
    logits[...] = logits_in[...]
    grad_out[...] = full[...].astype(F32).reshape(grad_out.shape)
    grad_in[...] = low[...].astype(F32).reshape(grad_in.shape[::-1]).T


def per_device(
    tile_values, tile_rows, tile_cols, tile_counts, features, weight_in, weight_out, cotangent
):
    hbm = pl.BlockSpec(memory_space=pltpu.HBM)
    block = pltpu.VMEM((BLOCKS, TILE, TILE), BF)
    dma = pltpu.SemaphoreType.DMA
    scratch = [block] * (2 * GROUPS)
    scratch += [pltpu.VMEM((GROUPS, NX, SLOTS, TILE, TILE), BF)] * 2
    scratch += [pltpu.VMEM((GROUPS, NX - 1, SLOTS, TILE, TILE), BF)] * 2
    scratch += [
        pltpu.VMEM((ND, SLOTS, TILE, TILE), BF),
        pltpu.VMEM((TILE, 512), BF),
        pltpu.VMEM((512, 512), BF),
        pltpu.VMEM((256, 512), BF),
        pltpu.SMEM((SLOTS, ND), jnp.int32),
        pltpu.SMEM((SLOTS, ND), jnp.int32),
        pltpu.SMEM((1, ND), jnp.int32),
        pltpu.VMEM((NX - 1, SLOTS, ND), jnp.int32),
        pltpu.SMEM((NX - 1, SLOTS, ND), jnp.int32),
        pltpu.VMEM((NX - 1, 1, ND), jnp.int32),
        pltpu.SMEM((NX - 1, 1, ND), jnp.int32),
        pltpu.VMEM((len(MOVED), NX - 1, SLOTS, TILE, TILE), BF),
        pltpu.VMEM((len(MOVED), NX - 1, 256, 256), BF),
        pltpu.VMEM((NX, SLOTS, TILE, TILE), BF),
        pltpu.VMEM((NX - 1, 256, TILE), F32),
        pltpu.VMEM((NX - 1, 256, TILE), BF),
        pltpu.VMEM((NX - 1, 256, TILE), BF),
        pltpu.VMEM((NX - 1, SLOTS, ND), jnp.int32),
        pltpu.SMEM((NX - 1, SLOTS, ND), jnp.int32),
        pltpu.VMEM((ND, 256, 256), BF),
        pltpu.VMEM((512, TILE), BF),
        pltpu.VMEM((512, 256), BF),
        pltpu.VMEM((256, TILE), F32),
        pltpu.VMEM((OWN, TILE, TILE), BF),
        pltpu.VMEM((512, 256), F32),
        pltpu.VMEM((512, TILE), F32),
        pltpu.VMEM((512, 256), BF),
        pltpu.VMEM((256, 512), BF),
        pltpu.VMEM((SHARE, CHUNK, LANES), BF),
        pltpu.VMEM((SHARE, CHUNK, LANES), BF),
        pltpu.VMEM((SHARE, CHUNK, WIDE), BF),
        pltpu.VMEM((PLANE - 1, CHUNK, WIDE), BF),
        pltpu.VMEM((NZ, CHUNK, WIDE), BF),
        pltpu.VMEM((CHUNKS, CHUNK, WIDE), BF),
        pltpu.VMEM((SHARE, CHUNK, TILE), BF),
        pltpu.VMEM((NZ - 1, 2, CHUNK, TILE), BF),
        pltpu.VMEM((PLANE, 2, CHUNK, TILE), BF),
        pltpu.VMEM((CHUNKS, CHUNK, TILE), BF),
    ]
    for shape in (
        (19,),
        (2, GROUPS),
        (2, len(EARLY), NY - 1),
        (2, STEPS),
        (2, GROUPS),
        (2, GROUPS),
        (NX - 1,),
    ):
        scratch.append(dma(shape))
    scratch += [dma((NX - 1,))] * 6
    scratch += [dma((1,)), dma((1,)), dma((8,)), dma((PLANE - 1,)), dma((11,))]
    logits, full, low = pl.pallas_call(
        kernel,
        out_shape=(
            jax.ShapeDtypeStruct((256, 512), BF),
            jax.ShapeDtypeStruct((CHUNKS, CHUNK, WIDE), BF),
            jax.ShapeDtypeStruct((CHUNKS, CHUNK, TILE), BF),
        ),
        in_specs=[hbm] * 8,
        out_specs=(hbm,) * 3,
        scratch_shapes=scratch,
        compiler_params=pltpu.CompilerParams(
            collective_id=0, has_side_effects=True, vmem_limit_bytes=60 * 1024 * 1024
        ),
        cost_estimate=pl.CostEstimate(
            flops=5_000_000_000, bytes_accessed=5_000_000, transcendentals=4_000_000
        ),
    )(
        tile_values.reshape(ND, SLOTS, TILE, TILE),
        tile_rows[0, 0].T,
        tile_cols[0, 0].T,
        tile_counts[0],
        features.reshape(OWN, TILE, TILE),
        weight_in,
        weight_out,
        cotangent,
    )
    return pl.pallas_call(
        unpack,
        out_shape=(
            jax.ShapeDtypeStruct((256, 512), BF),
            jax.ShapeDtypeStruct((TILE, 512), F32),
            jax.ShapeDtypeStruct((512, 512), F32),
        ),
        grid=(2,),
        in_specs=[
            pl.BlockSpec((128, 512), lambda i: (i, 0)),
            pl.BlockSpec((SHARE, CHUNK, WIDE), lambda i: (i, 0, 0)),
            pl.BlockSpec((SHARE, CHUNK, TILE), lambda i: (i, 0, 0)),
        ],
        out_specs=(
            pl.BlockSpec((128, 512), lambda i: (i, 0)),
            pl.BlockSpec((TILE, 256), lambda i: (0, i)),
            pl.BlockSpec((256, WIDE), lambda i: (i, 0)),
        ),
        compiler_params=pltpu.CompilerParams(vmem_limit_bytes=60 * 1024 * 1024),
    )(logits, full, low)


def solution(mesh):
    placed = (
        P("rep", "dom", None, None, None, None),
        P("rep", "dom", None, None),
        P("rep", "dom", None, None),
        P("rep", "dom", None),
        P(("dom", "rep"), None),
        P(),
        P(),
        P(("dom", "rep"), None),
    )
    return jax.shard_map(
        per_device,
        mesh=mesh,
        in_specs=placed,
        out_specs=(P(("dom", "rep"), None), P(), P()),
        check_vma=False,
    )
```
